32 devices in a mesh: fsdp: 8 (over z, y), ctx: 4 (over x, core).
Axes of the slice: x: 2, y: 2, z: 4, core: 2. Of those that a mesh axis runs over, the one named last changes fastest.
Arguments:
- tokens: bfloat16 [8, 512, 640], P('fsdp', 'ctx'), may hold values from -6 to 6
- positions: int32 [8, 512], P('fsdp', 'ctx'), may hold values from 0 to 511, as said below
- cotangent: bfloat16 [8, 512, 640], P('fsdp', 'ctx'), may hold values from -6 to 6
- attn_norm: bfloat16 [640], P('fsdp'), may hold values from 0.099609375 to 1.8984375
- w_query: bfloat16 [640, 1024], P('fsdp'), may hold values from -0.25 to 0.25
- w_key: bfloat16 [640, 256], P('fsdp'), may hold values from -0.25 to 0.25
- w_value: bfloat16 [640, 256], P('fsdp'), may hold values from -0.25 to 0.25
- query_norm: bfloat16 [256], P('fsdp'), may hold values from 0.099609375 to 1.8984375
- key_norm: bfloat16 [256], P('fsdp'), may hold values from 0.099609375 to 1.8984375
- w_output: bfloat16 [1024, 640], P('fsdp'), may hold values from -0.1875 to 0.1875
- attn_post_norm: bfloat16 [640], P('fsdp'), may hold values from 0.099609375 to 1.8984375
- ffn_norm: bfloat16 [640], P('fsdp'), may hold values from 0.099609375 to 1.8984375
- w_gate: bfloat16 [640, 2048], P('fsdp'), may hold values from -0.25 to 0.25
- w_up: bfloat16 [640, 2048], P('fsdp'), may hold values from -0.25 to 0.25
- w_down: bfloat16 [2048, 640], P('fsdp'), may hold values from -0.125 to 0.125
- ffn_post_norm: bfloat16 [640], P('fsdp'), may hold values from 0.099609375 to 1.8984375
Outputs:
- layer_out: bfloat16 [8, 512, 640], P('fsdp', 'ctx')
- tokens_grad: bfloat16 [8, 512, 640], P('fsdp', 'ctx')
- attn_norm_grad: float32 [640], P('fsdp')
- w_query_grad: float32 [640, 1024], P('fsdp')
- w_key_grad: float32 [640, 256], P('fsdp')
- w_value_grad: float32 [640, 256], P('fsdp')
- query_norm_grad: float32 [256], P('fsdp')
- key_norm_grad: float32 [256], P('fsdp')
- w_output_grad: float32 [1024, 640], P('fsdp')
- attn_post_norm_grad: float32 [640], P('fsdp')
- ffn_norm_grad: float32 [640], P('fsdp')
- w_gate_grad: float32 [640, 2048], P('fsdp')
- w_up_grad: float32 [640, 2048], P('fsdp')
- w_down_grad: float32 [2048, 640], P('fsdp')
- ffn_post_norm_grad: float32 [640], P('fsdp')
The draws below stay inside these ranges and needn't reach their ends.
Inputs may be any that keep to these rules, and one draw needn't show every extreme that they name: positions restart at 0 where a document begins and rise by one per token inside it; documents are consecutive runs of a sequence, so a token's position never exceeds its index in the sequence. Documents are mostly 200 to 2000 tokens, but a sequence's last document may be cut short, and one sequence starts and ends with documents of 1 to 63 tokens; some sequence is one whole document.
All inputs are finite; a program needn't handle non-finite values.
Results may differ from the reference program's by a relative error of at most 0.015.
Values may be sent and summed in bfloat16 or wider, within the bound.
A program may use at most 128 MiB of HBM per device.

```python
import jax
import jax.numpy as jnp
from jax import lax

D = 640
HQ = 4
HD = 256
FF = 2048
WINDOW = 512
TOK_DEV = 128
MIN_DOC = 200
MAX_DOC = 2000
SEQ_LEN = 512
SEQS = 8


def draw_positions(key, part):
    key = jax.random.fold_in(key, 11)
    key_len, key_pick, key_head, key_tail = jax.random.split(key, 4)
    count = SEQ_LEN // MIN_DOC + 2
    lengths = jax.random.randint(key_len, (SEQS, count), MIN_DOC, MAX_DOC + 1)
    chosen = jax.random.randint(key_pick, (), 0, SEQS)
    whole_row = (chosen + 1) % SEQS
    row_index = jnp.arange(SEQS, dtype=jnp.int32)[:, None]
    column_index = jnp.arange(count, dtype=jnp.int32)[None, :]
    lengths = jnp.where((row_index == whole_row) & (column_index == 0), SEQ_LEN, lengths)
    ends = jnp.cumsum(lengths, axis=1)
    starts = ends - lengths
    head_len = jax.random.randint(key_head, (SEQS, 1), 1, max(TOK_DEV // 2, 2))
    tail_len = jax.random.randint(key_tail, (SEQS, 1), 1, max(TOK_DEV // 2, 2))
    span_starts = jnp.concatenate([jnp.zeros((SEQS, 1), jnp.int32), head_len.astype(jnp.int32), (SEQ_LEN - tail_len).astype(jnp.int32), jnp.full((SEQS, count - 3), SEQ_LEN, jnp.int32)], axis=1)
    picked = row_index == chosen
    starts = jnp.where(picked, span_starts, starts.astype(jnp.int32))
    token_index = jnp.arange(SEQ_LEN, dtype=jnp.int32)
    before = starts[:, None, :] <= token_index[None, :, None]
    doc_start = jnp.max(jnp.where(before, starts[:, None, :], 0), axis=-1)
    return (token_index[None, :] - doc_start).astype(jnp.int32)


def shard_levels(rng, dims, cuts, low, top_value):
    def one(axis_at, blocks):
        draws = jax.random.uniform(jax.random.fold_in(jax.random.fold_in(rng, 6), axis_at), (blocks,), jnp.float32, low / len(cuts), top_value / len(cuts))
        return jnp.repeat(jnp.exp(draws), dims[axis_at] // blocks).reshape((-1,) + (1,) * (len(dims) - axis_at - 1))

    loudness = one(*cuts[0])
    for cut in cuts[1:]:
        loudness = loudness * one(*cut)
    return loudness


def bell_draw(own_key, dims, deviation, bound, cuts=(), kind=jnp.bfloat16):
    level = shard_levels(own_key, dims, cuts, -0.22, 0.18) if cuts else 1.0
    result = jax.random.normal(own_key, dims, jnp.float32) * deviation * level
    return jnp.minimum(jnp.maximum(result, -bound), bound).astype(kind)


def setup_inputs(seed: int = 0) -> dict:
    seeds = jax.random.split(jax.random.key(seed), 17)
    return {
        "tokens": bell_draw(seeds[0], (SEQS, SEQ_LEN, D), 1.0, 6.0, ((0, 8), (1, 4))),
        "positions": draw_positions(jax.random.fold_in(seeds[16], 71), 0),
        "cotangent": bell_draw(seeds[2], (SEQS, SEQ_LEN, D), 1.0, 6.0, ((0, 8), (1, 4))),
        "attn_norm": jnp.clip(1.0 + 0.18 * jax.random.normal(seeds[3], (D,), jnp.float32), 0.099609375, 1.8984375).astype(jnp.bfloat16),
        "w_query": bell_draw(seeds[4], (D, HQ * HD), D ** -0.5, 0.25, ((0, 8),)),
        "w_key": bell_draw(seeds[5], (D, HD), D ** -0.5, 0.25, ((0, 8),)),
        "w_value": bell_draw(seeds[6], (D, HD), D ** -0.5, 0.25, ((0, 8),)),
        "query_norm": jnp.clip(1.0 + 0.18 * jax.random.normal(seeds[7], (HD,), jnp.float32), 0.099609375, 1.8984375).astype(jnp.bfloat16),
        "key_norm": jnp.clip(1.0 + 0.18 * jax.random.normal(seeds[8], (HD,), jnp.float32), 0.099609375, 1.8984375).astype(jnp.bfloat16),
        "w_output": bell_draw(seeds[9], (HQ * HD, D), (HQ * HD) ** -0.5, 0.1875, ((0, 8),)),
        "attn_post_norm": jnp.clip(1.0 + 0.18 * jax.random.normal(seeds[10], (D,), jnp.float32), 0.099609375, 1.8984375).astype(jnp.bfloat16),
        "ffn_norm": jnp.clip(1.0 + 0.18 * jax.random.normal(seeds[11], (D,), jnp.float32), 0.099609375, 1.8984375).astype(jnp.bfloat16),
        "w_gate": bell_draw(seeds[12], (D, FF), D ** -0.5, 0.25, ((0, 8),)),
        "w_up": bell_draw(seeds[13], (D, FF), D ** -0.5, 0.25, ((0, 8),)),
        "w_down": bell_draw(seeds[14], (FF, D), FF ** -0.5, 0.125, ((0, 8),)),
        "ffn_post_norm": jnp.clip(1.0 + 0.18 * jax.random.normal(seeds[15], (D,), jnp.float32), 0.099609375, 1.8984375).astype(jnp.bfloat16),
    }


EPSILON = 1e-06
ATTN_SCALE = 0.0625
NEGATIVE = -1e+30

@jax.custom_vjp
def low(v):
    return lax.optimization_barrier(v.astype(jnp.bfloat16)).astype(jnp.float32)

@jax.custom_vjp
def low_back(v):
    return v

def low_keep(v):
    return (low(v), None)

def low_pass(kept, grad):
    return (grad,)

def back_keep(v):
    return (v, None)

def back_low(kept, grad):
    return (low(grad),)
low.defvjp(low_keep, low_pass)
low_back.defvjp(back_keep, back_low)

def rms_gain(values, gain_vec):
    return values * lax.rsqrt(lax.optimization_barrier(jnp.mean(values * values, axis=-1, keepdims=True)) + EPSILON) * gain_vec

def rope_tables(seq_place):
    half_width = HD // 2
    inverse = jnp.power(10000.0, -jnp.arange(half_width, dtype=jnp.float32) * (2.0 / HD))
    angles = seq_place.astype(jnp.float32)[:, None] * inverse[None, :]
    return (jnp.cos(angles)[:, None, :], jnp.sin(angles)[:, None, :])

def rotate(values, cosine, sine_table):
    half_width = values.shape[-1] // 2
    front_half = values[..., :half_width]
    back_half = values[..., half_width:]
    return jnp.concatenate([front_half * cosine - back_half * sine_table, back_half * cosine + front_half * sine_table], axis=-1)

def query_key(q_pre, k_pre, g_query, g_key, cosine, sine_table):
    return (rotate(rms_gain(q_pre, g_query), cosine, sine_table), rotate(rms_gain(k_pre, g_key), cosine, sine_table))

def gated_gelu(gate_proj, up_proj):
    return jax.nn.gelu(gate_proj, approximate=True) * up_proj

def one_sequence(seq_tokens, seq_place, params):
    g_attn, wq_full, wk_full, wv_full, gq_full, gk_full, wo_full, g_attn_post, g_ffn, wg_full, wu_full, wd_full, g_ffn_post = params
    highest = lax.Precision.HIGHEST
    normed = low(rms_gain(seq_tokens, g_attn))
    q_pre = low_back(jnp.dot(normed, wq_full, precision=highest)).reshape(SEQ_LEN, HQ, HD)
    k_pre = low_back(jnp.dot(normed, wk_full, precision=highest)).reshape(SEQ_LEN, 1, HD)
    v_rows = low_back(low(jnp.dot(normed, wv_full, precision=highest)))
    cosine, sine_table = rope_tables(seq_place)
    q_turned, k_turned = query_key(q_pre, k_pre, gq_full, gk_full, cosine, sine_table)
    q_rows = low(q_turned)
    k_rows = low(k_turned.reshape(SEQ_LEN, HD))
    k_padded = jnp.concatenate([jnp.zeros((WINDOW, HD), k_rows.dtype), k_rows], axis=0)
    v_padded = jnp.concatenate([jnp.zeros((WINDOW, HD), v_rows.dtype), v_rows], axis=0)
    block_rows = min(512, SEQ_LEN)

    def attend(block_index):
        row_start = (block_index * block_rows).astype(jnp.int32)
        q_block = lax.dynamic_slice_in_dim(q_rows, row_start, block_rows, 0)
        k_block = lax.dynamic_slice_in_dim(k_padded, row_start, block_rows + WINDOW, 0)
        v_block = lax.dynamic_slice_in_dim(v_padded, row_start, block_rows + WINDOW, 0)
        place_block = lax.dynamic_slice_in_dim(seq_place, row_start, block_rows, 0)
        q_index = row_start + jnp.arange(block_rows, dtype=jnp.int32)
        k_index = row_start - WINDOW + jnp.arange(block_rows + WINDOW, dtype=jnp.int32)
        key_mask = (k_index[None, :] <= q_index[:, None]) & (q_index[:, None] - k_index[None, :] < WINDOW) & (k_index[None, :] >= (q_index - place_block)[:, None])
        raw_scores = jnp.einsum('qhd,kd->hqk', q_block, k_block, precision=highest) * ATTN_SCALE
        scores = jnp.where(key_mask[None], low_back(raw_scores), NEGATIVE)
        row_max = lax.optimization_barrier(jnp.max(scores, axis=-1, keepdims=True))
        shifted = jnp.exp(scores - row_max)
        prob_rows = shifted / lax.optimization_barrier(jnp.sum(shifted, axis=-1, keepdims=True))
        return jnp.einsum('hqk,kd->qhd', low(prob_rows), v_block, precision=highest)
    blocks = lax.map(jax.checkpoint(attend), jnp.arange(SEQ_LEN // block_rows, dtype=jnp.int32))
    attended = low_back(low(blocks.reshape(SEQ_LEN, HQ * HD)))
    branch = low_back(jnp.dot(attended, wo_full, precision=highest))
    hidden_res = seq_tokens + rms_gain(branch, g_attn_post)
    ffn_in = low(rms_gain(hidden_res, g_ffn))
    gate_proj = low_back(jnp.dot(ffn_in, wg_full, precision=highest))
    up_proj = low_back(jnp.dot(ffn_in, wu_full, precision=highest))
    mixed = low(gated_gelu(gate_proj, up_proj))
    down_out = low_back(jnp.dot(mixed, wd_full, precision=highest))
    return hidden_res + rms_gain(down_out, g_ffn_post)

def reference(tokens, positions, cotangent, attn_norm, w_query, w_key, w_value, query_norm, key_norm, w_output, attn_post_norm, ffn_norm, w_gate, w_up, w_down, ffn_post_norm):
    params = tuple((weight_item.astype(jnp.float32) for weight_item in (attn_norm, w_query, w_key, w_value, query_norm, key_norm, w_output, attn_post_norm, ffn_norm, w_gate, w_up, w_down, ffn_post_norm)))

    def forward(seq_all, param_all):

        def per_sequence(seq_pair):
            return one_sequence(seq_pair[0], seq_pair[1], param_all)
        return lax.map(jax.checkpoint(per_sequence), (seq_all, positions))
    layer_out, pull_back = jax.vjp(forward, tokens.astype(jnp.float32), params)
    d_tokens, d_params = pull_back(cotangent.astype(jnp.float32))
    return (layer_out.astype(jnp.bfloat16), d_tokens.astype(jnp.bfloat16), d_params[0], d_params[1], d_params[2], d_params[3], d_params[4], d_params[5], d_params[6], d_params[7], d_params[8], d_params[9], d_params[10], d_params[11], d_params[12])
```

```python
import functools

import jax
import jax.numpy as jnp
from jax import lax
from jax.experimental import pallas as pl
from jax.experimental.pallas import tpu as pltpu
from jax.sharding import PartitionSpec as P

HQ = 4
HD = 256
WINDOW = 512


EPSILON = 1e-06
ATTN_SCALE = 0.0625
NEGATIVE = -1e30


def shifted_2(value, axis, steps):
    count = lax.axis_size(axis)
    leading, last = (max(0, -steps), min(count, count - steps))
    return lax.ppermute(value, axis, [(source, source + steps) for source in range(leading, last)])


def rms_gain(values, gain_vec):
    return (
        values * lax.rsqrt(jnp.mean(values * values, axis=-1, keepdims=True) + EPSILON) * gain_vec
    )


def rope_tables(seq_place):
    half_width = HD // 2
    inverse = jnp.power(10000.0, -jnp.arange(half_width, dtype=jnp.float32) * (2.0 / HD))
    angles = seq_place.astype(jnp.float32)[:, None] * inverse[None, :]
    return (jnp.cos(angles)[:, None, :], jnp.sin(angles)[:, None, :])


def rotate(values, cosine, sine_table):
    half_width = values.shape[-1] // 2
    front_half = values[..., :half_width]
    back_half = values[..., half_width:]
    return jnp.concatenate(
        [
            front_half * cosine - back_half * sine_table,
            back_half * cosine + front_half * sine_table,
        ],
        axis=-1,
    )


def query_key(q_pre, k_pre, g_query, g_key, cosine, sine_table):
    return (
        rotate(rms_gain(q_pre, g_query), cosine, sine_table),
        rotate(rms_gain(k_pre, g_key), cosine, sine_table),
    )


def gated_gelu(gate_proj, up_proj):
    return jax.nn.gelu(gate_proj, approximate=True) * up_proj


def masked_scores(q_low, key_rows, key_mask):
    raw_scores = (
        jnp.einsum("thd,kd->htk", q_low, key_rows, preferred_element_type=jnp.float32) * ATTN_SCALE
    )
    return jnp.where(key_mask[None], raw_scores, NEGATIVE)


def plain_body(
    tokens,
    positions,
    cotangent,
    attn_norm,
    w_query,
    w_key,
    w_value,
    query_norm,
    key_norm,
    w_output,
    attn_post_norm,
    ffn_norm,
    w_gate,
    w_up,
    w_down,
    ffn_post_norm,
):
    f32 = jnp.float32
    bf16 = jnp.bfloat16
    tok_rows = tokens.shape[1]
    model_width = tokens.shape[2]
    inputs = tokens.reshape(tok_rows, model_width).astype(f32)
    grad_out = cotangent.reshape(tok_rows, model_width).astype(f32)
    seq_place = positions.reshape(tok_rows)
    g_attn, wq_full, wk_full, wv_full, gq_full, gk_full, wo_full, g_attn_post = (
        lax.all_gather(attn_norm, "fsdp", axis=0, tiled=True),
        lax.all_gather(w_query, "fsdp", axis=0, tiled=True),
        lax.all_gather(w_key, "fsdp", axis=0, tiled=True),
        lax.all_gather(w_value, "fsdp", axis=0, tiled=True),
        lax.all_gather(query_norm, "fsdp", axis=0, tiled=True),
        lax.all_gather(key_norm, "fsdp", axis=0, tiled=True),
        lax.all_gather(w_output, "fsdp", axis=0, tiled=True),
        lax.all_gather(attn_post_norm, "fsdp", axis=0, tiled=True),
    )
    block_index = lax.axis_index("ctx")
    halo_count = -(-WINDOW // tok_rows)
    query_index = block_index * tok_rows + jnp.arange(tok_rows, dtype=jnp.int32)
    key_index = block_index * tok_rows + jnp.arange(
        -halo_count * tok_rows, tok_rows, dtype=jnp.int32
    )
    key_mask = (
        (key_index[None, :] <= query_index[:, None])
        & (query_index[:, None] - key_index[None, :] < WINDOW)
        & (key_index[None, :] >= (query_index - seq_place)[:, None])
    )
    attn_in = rms_gain(inputs, g_attn.astype(f32)).astype(bf16)
    q_pre = jnp.dot(attn_in, wq_full, preferred_element_type=f32).reshape(tok_rows, HQ, HD)
    k_pre = jnp.dot(attn_in, wk_full, preferred_element_type=f32).reshape(tok_rows, 1, HD)
    v_low = jnp.dot(attn_in, wv_full, preferred_element_type=f32).astype(bf16)
    cosine, sine_table = rope_tables(seq_place)
    gq_gain = gq_full.astype(f32)
    gk_gain = gk_full.astype(f32)
    q_turned, k_turned = query_key(q_pre, k_pre, gq_gain, gk_gain, cosine, sine_table)
    q_low = q_turned.astype(bf16)
    k_low = k_turned.reshape(tok_rows, HD).astype(bf16)
    key_parts = []
    value_parts = []
    for distance in range(halo_count, 0, -1):
        got_keys, got_values = shifted_2((k_low, v_low), "ctx", distance)
        key_parts.append(got_keys)
        value_parts.append(got_values)
    key_rows = jnp.concatenate(key_parts + [k_low], axis=0)
    value_rows = jnp.concatenate(value_parts + [v_low], axis=0)
    scores = masked_scores(q_low, key_rows, key_mask)
    row_max = jnp.max(scores, axis=-1, keepdims=True)
    shifted = jnp.exp(scores - row_max)
    row_total = jnp.sum(shifted, axis=-1, keepdims=True)
    log_total = row_max + jnp.log(row_total)
    prob_low = (shifted / row_total).astype(bf16)
    attended = jnp.einsum("htk,kd->thd", prob_low, value_rows, preferred_element_type=f32)
    att_low = attended.reshape(tok_rows, HQ * HD).astype(bf16)
    attn_branch = jnp.dot(att_low, wo_full, preferred_element_type=f32)
    g_post_gain = g_attn_post.astype(f32)
    hidden_res = inputs + rms_gain(attn_branch, g_post_gain)
    g_ffn, wg_full, wu_full, wd_full, g_ffn_post = (
        lax.all_gather(ffn_norm, "fsdp", axis=0, tiled=True),
        lax.all_gather(w_gate, "fsdp", axis=0, tiled=True),
        lax.all_gather(w_up, "fsdp", axis=0, tiled=True),
        lax.all_gather(w_down, "fsdp", axis=0, tiled=True),
        lax.all_gather(ffn_post_norm, "fsdp", axis=0, tiled=True),
    )
    g_ffn_gain = g_ffn.astype(f32)
    g_ffn_post_gain = g_ffn_post.astype(f32)
    ffn_in = rms_gain(hidden_res, g_ffn_gain).astype(bf16)
    gate_proj = jnp.dot(ffn_in, wg_full, preferred_element_type=f32)
    up_proj = jnp.dot(ffn_in, wu_full, preferred_element_type=f32)
    mixed_low = gated_gelu(gate_proj, up_proj).astype(bf16)
    down_out = jnp.dot(mixed_low, wd_full, preferred_element_type=f32)
    layer_out = hidden_res + rms_gain(down_out, g_ffn_post_gain)
    g_ffn, wg_full, wu_full, wd_full, g_ffn_post = (
        lax.all_gather(ffn_norm, "fsdp", axis=0, tiled=True),
        lax.all_gather(w_gate, "fsdp", axis=0, tiled=True),
        lax.all_gather(w_up, "fsdp", axis=0, tiled=True),
        lax.all_gather(w_down, "fsdp", axis=0, tiled=True),
        lax.all_gather(ffn_post_norm, "fsdp", axis=0, tiled=True),
    )
    unused, post_ffn_back = jax.vjp(rms_gain, down_out, g_ffn_post_gain)
    d_down, d_ffn_post = post_ffn_back(grad_out)
    d_down_low = d_down.astype(bf16)
    grad_w_down = jnp.einsum("tf,td->fd", mixed_low, d_down_low, preferred_element_type=f32)
    d_mixed = jnp.einsum("td,fd->tf", d_down_low, wd_full, preferred_element_type=f32)
    unused, glu_back = jax.vjp(gated_gelu, gate_proj, up_proj)
    d_gate, d_up = glu_back(d_mixed)
    d_gate_low = d_gate.astype(bf16)
    d_up_low = d_up.astype(bf16)
    grad_w_gate = jnp.einsum("td,tf->df", ffn_in, d_gate_low, preferred_element_type=f32)
    grad_w_up = jnp.einsum("td,tf->df", ffn_in, d_up_low, preferred_element_type=f32)
    d_ffn_in = jnp.einsum(
        "tf,df->td", d_gate_low, wg_full, preferred_element_type=f32
    ) + jnp.einsum("tf,df->td", d_up_low, wu_full, preferred_element_type=f32)
    unused, ffn_norm_back = jax.vjp(rms_gain, hidden_res, g_ffn_gain)
    d_hidden_part, d_ffn_norm = ffn_norm_back(d_ffn_in)
    d_hidden = grad_out + d_hidden_part
    ffn_sums = (
        lax.psum_scatter(d_ffn_norm, "fsdp", scatter_dimension=0, tiled=True),
        lax.psum_scatter(grad_w_gate, "fsdp", scatter_dimension=0, tiled=True),
        lax.psum_scatter(grad_w_up, "fsdp", scatter_dimension=0, tiled=True),
        lax.psum_scatter(grad_w_down, "fsdp", scatter_dimension=0, tiled=True),
        lax.psum_scatter(d_ffn_post, "fsdp", scatter_dimension=0, tiled=True),
    )
    g_attn, wq_full, wk_full, wv_full, gq_full, gk_full, wo_full, g_attn_post = (
        lax.all_gather(attn_norm, "fsdp", axis=0, tiled=True),
        lax.all_gather(w_query, "fsdp", axis=0, tiled=True),
        lax.all_gather(w_key, "fsdp", axis=0, tiled=True),
        lax.all_gather(w_value, "fsdp", axis=0, tiled=True),
        lax.all_gather(query_norm, "fsdp", axis=0, tiled=True),
        lax.all_gather(key_norm, "fsdp", axis=0, tiled=True),
        lax.all_gather(w_output, "fsdp", axis=0, tiled=True),
        lax.all_gather(attn_post_norm, "fsdp", axis=0, tiled=True),
    )
    unused, post_attn_back = jax.vjp(rms_gain, attn_branch, g_post_gain)
    d_branch, d_attn_post = post_attn_back(d_hidden)
    d_branch_low = d_branch.astype(bf16)
    grad_w_output = jnp.einsum("tc,td->cd", att_low, d_branch_low, preferred_element_type=f32)
    d_attended = (
        jnp.einsum("td,cd->tc", d_branch_low, wo_full, preferred_element_type=f32)
        .reshape(tok_rows, HQ, HD)
        .astype(bf16)
    )
    scores = masked_scores(q_low, key_rows, key_mask)
    prob_rows = jnp.exp(scores - log_total)
    prob_low = prob_rows.astype(bf16)
    d_values = jnp.einsum("htk,thd->kd", prob_low, d_attended, preferred_element_type=f32)
    d_probs = jnp.einsum("thd,kd->htk", d_attended, value_rows, preferred_element_type=f32)
    d_scores = prob_rows * (d_probs - jnp.sum(prob_rows * d_probs, axis=-1, keepdims=True))
    d_scores_low = d_scores.astype(bf16)
    d_queries = (
        jnp.einsum("htk,kd->thd", d_scores_low, key_rows, preferred_element_type=f32) * ATTN_SCALE
    )
    d_keys = jnp.einsum("htk,thd->kd", d_scores_low, q_low, preferred_element_type=f32) * ATTN_SCALE
    own_keys = d_keys[halo_count * tok_rows :]
    own_values = d_values[halo_count * tok_rows :]
    for distance in range(halo_count, 0, -1):
        part_index = halo_count - distance
        back_keys, back_values = shifted_2(
            (
                d_keys[part_index * tok_rows : (part_index + 1) * tok_rows],
                d_values[part_index * tok_rows : (part_index + 1) * tok_rows],
            ),
            "ctx",
            -distance,
        )
        own_keys = own_keys + back_keys
        own_values = own_values + back_values
    unused, turn_back = jax.vjp(
        lambda q_in, k_in, gq_in, gk_in: query_key(q_in, k_in, gq_in, gk_in, cosine, sine_table),
        q_pre,
        k_pre,
        gq_gain,
        gk_gain,
    )
    d_q_pre, d_k_pre, d_query_norm, d_key_norm = turn_back(
        (d_queries, own_keys.reshape(tok_rows, 1, HD))
    )
    dq_low = d_q_pre.reshape(tok_rows, HQ * HD).astype(bf16)
    dk_low = d_k_pre.reshape(tok_rows, HD).astype(bf16)
    dv_low = own_values.astype(bf16)
    grad_w_query = jnp.einsum("td,tc->dc", attn_in, dq_low, preferred_element_type=f32)
    grad_w_key = jnp.einsum("td,tc->dc", attn_in, dk_low, preferred_element_type=f32)
    grad_w_value = jnp.einsum("td,tc->dc", attn_in, dv_low, preferred_element_type=f32)
    d_attn_in = (
        jnp.einsum("tc,dc->td", dq_low, wq_full, preferred_element_type=f32)
        + jnp.einsum("tc,dc->td", dk_low, wk_full, preferred_element_type=f32)
        + jnp.einsum("tc,dc->td", dv_low, wv_full, preferred_element_type=f32)
    )
    unused, first_back = jax.vjp(rms_gain, inputs, g_attn.astype(f32))
    d_inputs_part, d_attn_norm = first_back(d_attn_in)
    d_tokens = d_hidden + d_inputs_part
    attn_sums = (
        lax.psum_scatter(d_attn_norm, "fsdp", scatter_dimension=0, tiled=True),
        lax.psum_scatter(grad_w_query, "fsdp", scatter_dimension=0, tiled=True),
        lax.psum_scatter(grad_w_key, "fsdp", scatter_dimension=0, tiled=True),
        lax.psum_scatter(grad_w_value, "fsdp", scatter_dimension=0, tiled=True),
        lax.psum_scatter(d_query_norm, "fsdp", scatter_dimension=0, tiled=True),
        lax.psum_scatter(d_key_norm, "fsdp", scatter_dimension=0, tiled=True),
        lax.psum_scatter(grad_w_output, "fsdp", scatter_dimension=0, tiled=True),
        lax.psum_scatter(d_attn_post, "fsdp", scatter_dimension=0, tiled=True),
    )
    column_sums = (
        lax.psum_scatter(attn_sums[1], "ctx", scatter_dimension=1, tiled=True),
        lax.psum_scatter(attn_sums[2], "ctx", scatter_dimension=1, tiled=True),
        lax.psum_scatter(attn_sums[3], "ctx", scatter_dimension=1, tiled=True),
        lax.psum_scatter(attn_sums[6], "ctx", scatter_dimension=1, tiled=True),
        lax.psum_scatter(ffn_sums[1], "ctx", scatter_dimension=1, tiled=True),
        lax.psum_scatter(ffn_sums[2], "ctx", scatter_dimension=1, tiled=True),
        lax.psum_scatter(ffn_sums[3], "ctx", scatter_dimension=1, tiled=True),
    )
    full_columns = (
        lax.all_gather(column_sums[0], "ctx", axis=1, tiled=True),
        lax.all_gather(column_sums[1], "ctx", axis=1, tiled=True),
        lax.all_gather(column_sums[2], "ctx", axis=1, tiled=True),
        lax.all_gather(column_sums[3], "ctx", axis=1, tiled=True),
        lax.all_gather(column_sums[4], "ctx", axis=1, tiled=True),
        lax.all_gather(column_sums[5], "ctx", axis=1, tiled=True),
        lax.all_gather(column_sums[6], "ctx", axis=1, tiled=True),
    )
    gain_totals = lax.psum(
        (attn_sums[0], attn_sums[4], attn_sums[5], attn_sums[7], ffn_sums[0], ffn_sums[4]), "ctx"
    )
    results = (
        gain_totals[0],
        full_columns[0],
        full_columns[1],
        full_columns[2],
        gain_totals[1],
        gain_totals[2],
        full_columns[3],
        gain_totals[3],
        gain_totals[4],
        full_columns[4],
        full_columns[5],
        full_columns[6],
        gain_totals[5],
    )
    out_rows = layer_out.astype(bf16).reshape(1, tok_rows, model_width)
    grad_rows = d_tokens.astype(bf16).reshape(1, tok_rows, model_width)
    return (
        out_rows,
        grad_rows,
        results[0],
        results[1],
        results[2],
        results[3],
        results[4],
        results[5],
        results[6],
        results[7],
        results[8],
        results[9],
        results[10],
        results[11],
        results[12],
    )


VMEM_BYTES = 48 * 1024 * 1024


def peer_of(axis, index):
    return dict(device_id={axis: index}, device_id_type=pl.DeviceIdType.MESH)


def greet(axis, indices):
    barrier = pltpu.get_barrier_semaphore()
    for index in indices:
        pl.semaphore_signal(barrier, inc=1, **peer_of(axis, index))
    pl.semaphore_wait(barrier, len(indices))


def gather_kernel(axis, n, count, *refs):
    ins, outs = refs[:count], refs[count : 2 * count]
    send, recv = refs[2 * count :]
    me = lax.axis_index(axis)
    outer, inner = lax.div(me, 2), lax.rem(me, 2)
    span = n // 2
    twin = outer * 2 + (1 - inner)

    def ahead(step):
        return lax.rem(outer + step, span) * 2 + inner

    def behind(step):
        return lax.rem(outer + span - step, span)

    greet(axis, [twin] + [ahead(step) for step in range(1, span)])

    def copy(i, source, slot, lane, target):
        return pltpu.make_async_remote_copy(
            src_ref=source,
            dst_ref=outs[i].at[slot],
            send_sem=send.at[i, lane],
            recv_sem=recv.at[i, lane],
            **peer_of(axis, target),
        )

    for i in range(count):
        for step in range(1, span):
            copy(i, ins[i], me, step, ahead(step)).start()
        copy(i, ins[i], me, 0, twin).start()
    for i in range(count):
        outs[i][me] = ins[i][...]
    for i in range(count):
        for step in range(1, span):
            slot = behind(step) * 2 + inner
            copy(i, ins[i], slot, step, twin).wait_recv()
            copy(i, outs[i].at[slot], slot, span - 1 + step, twin).start()
    for i in range(count):
        copy(i, ins[i], twin, 0, twin).wait_recv()
        for step in range(1, span):
            slot = behind(step) * 2 + (1 - inner)
            copy(i, ins[i], slot, span - 1 + step, twin).wait_recv()
        for lane in range(2 * span - 1):
            copy(i, ins[i], me, lane, twin).wait_send()


def gather(axis, n, key, *arrays):
    count = len(arrays)
    spec = pl.BlockSpec(memory_space=pltpu.VMEM)
    return pl.pallas_call(
        functools.partial(gather_kernel, axis, n, count),
        out_shape=[jax.ShapeDtypeStruct((n,) + a.shape, a.dtype) for a in arrays],
        in_specs=[spec] * count,
        out_specs=[spec] * count,
        scratch_shapes=[
            pltpu.SemaphoreType.DMA((count, n - 1)),
            pltpu.SemaphoreType.DMA((count, n - 1)),
        ],
        compiler_params=pltpu.CompilerParams(
            collective_id=key, has_side_effects=True, vmem_limit_bytes=VMEM_BYTES
        ),
    )(*arrays)


def add_scatter_kernel(axis, n, count, *refs):
    ins, outs = refs[:count], refs[count : 2 * count]
    from_twin, paired, landed = (
        refs[2 * count : 3 * count],
        refs[3 * count : 4 * count],
        refs[4 * count : 5 * count],
    )
    send, recv = refs[5 * count :]
    me = lax.axis_index(axis)
    outer, inner = lax.div(me, 2), lax.rem(me, 2)
    span = n // 2
    twin = outer * 2 + (1 - inner)
    f32 = jnp.float32

    def ahead(step):
        return lax.rem(outer + step, span)

    greet(axis, [twin] + [ahead(step) * 2 + inner for step in range(1, span)])

    def to_twin(i, step):
        return pltpu.make_async_remote_copy(
            src_ref=ins[i].at[ahead(step) * 2 + (1 - inner)],
            dst_ref=from_twin[i].at[step],
            send_sem=send.at[i, step],
            recv_sem=recv.at[i, step],
            **peer_of(axis, twin),
        )

    def to_owner(i, step):
        return pltpu.make_async_remote_copy(
            src_ref=paired[i].at[step],
            dst_ref=landed[i].at[step],
            send_sem=send.at[i, span + step],
            recv_sem=recv.at[i, span + step],
            **peer_of(axis, ahead(step) * 2 + inner),
        )

    order = list(range(1, span)) + [0]
    for i in range(count):
        for step in order:
            to_twin(i, step).start()
    for i in range(count):
        for step in range(1, span):
            to_twin(i, step).wait_recv()
            paired[i][step] = (
                ins[i][ahead(step) * 2 + inner].astype(f32) + from_twin[i][step].astype(f32)
            ).astype(paired[i].dtype)
            to_owner(i, step).start()
    for i in range(count):
        to_twin(i, 0).wait_recv()
        total = ins[i][me].astype(f32) + from_twin[i][0].astype(f32)
        for step in range(1, span):
            to_owner(i, step).wait_recv()
            total = total + landed[i][step].astype(f32)
        outs[i][...] = total.astype(outs[i].dtype)
    for i in range(count):
        for step in range(span):
            to_twin(i, step).wait_send()
        for step in range(1, span):
            to_owner(i, step).wait_send()


def add_scatter(axis, n, key, out_type, *arrays):
    count = len(arrays)
    spec = pl.BlockSpec(memory_space=pltpu.VMEM)
    slots = [pltpu.VMEM((n // 2,) + a.shape[1:], a.dtype) for a in arrays]
    return pl.pallas_call(
        functools.partial(add_scatter_kernel, axis, n, count),
        out_shape=[jax.ShapeDtypeStruct(a.shape[1:], out_type) for a in arrays],
        in_specs=[spec] * count,
        out_specs=[spec] * count,
        scratch_shapes=slots * 3
        + [
            pltpu.SemaphoreType.DMA((count, n)),
            pltpu.SemaphoreType.DMA((count, n)),
        ],
        compiler_params=pltpu.CompilerParams(
            collective_id=key, has_side_effects=True, vmem_limit_bytes=VMEM_BYTES
        ),
    )(*arrays)


def swap_kernel(axis, n, in_ref, out_ref, send, recv):
    me = lax.axis_index(axis)

    def ahead(step):
        return lax.rem(me + step, n)

    greet(axis, [ahead(step) for step in range(1, n)])

    def copy(step, slot):
        return pltpu.make_async_remote_copy(
            src_ref=in_ref.at[ahead(step)],
            dst_ref=out_ref.at[slot],
            send_sem=send.at[step],
            recv_sem=recv.at[step],
            **peer_of(axis, ahead(step)),
        )

    for step in range(1, n):
        copy(step, me).start()
    out_ref[me] = in_ref[me]
    for step in range(1, n):
        copy(step, lax.rem(me + n - step, n)).wait_recv()
    for step in range(1, n):
        copy(step, me).wait_send()


def swap(axis, n, key, array):
    spec = pl.BlockSpec(memory_space=pltpu.VMEM)
    return pl.pallas_call(
        functools.partial(swap_kernel, axis, n),
        out_shape=jax.ShapeDtypeStruct(array.shape, array.dtype),
        in_specs=[spec],
        out_specs=spec,
        scratch_shapes=[pltpu.SemaphoreType.DMA((n,)), pltpu.SemaphoreType.DMA((n,))],
        compiler_params=pltpu.CompilerParams(
            collective_id=key, has_side_effects=True, vmem_limit_bytes=VMEM_BYTES
        ),
    )(array)


def turned_norm(values, gain_vec, cosine, sine_table):
    return rotate(rms_gain(values, gain_vec), cosine, sine_table)


def split_body(
    tokens,
    positions,
    cotangent,
    attn_norm,
    w_query,
    w_key,
    w_value,
    query_norm,
    key_norm,
    w_output,
    attn_post_norm,
    ffn_norm,
    w_gate,
    w_up,
    w_down,
    ffn_post_norm,
):
    f32 = jnp.float32
    bf16 = jnp.bfloat16
    ways = lax.axis_size("ctx")
    owners = lax.axis_size("fsdp")
    part = lax.axis_index("ctx")
    rows, width = tokens.shape[1:]
    seq = rows * ways
    shard = w_query.shape[0]
    hidden_row = w_down.shape[0] // ways
    out_row = w_output.shape[0] // ways
    head_share = query_norm.shape[0]
    inputs = tokens.reshape(rows, width).astype(f32)
    grad_out = cotangent.reshape(rows, width).astype(f32)

    def mul(left, right, dims):
        return lax.dot_general(left, right, (dims, ((), ())), preferred_element_type=f32)

    def nn(left, right):
        return mul(left, right, ((1,), (0,)))

    def nt(left, right):
        return mul(left, right, ((1,), (1,)))

    def tn(left, right):
        return mul(left, right, ((0,), (0,)))

    def hidden_part(weight):
        cut = weight.reshape(shard, owners, ways, hidden_row)
        return lax.dynamic_index_in_dim(cut, part, 2, keepdims=False).reshape(
            shard, owners * hidden_row
        )

    def hidden_whole(parts):
        return (
            parts.reshape(ways, shard, owners, hidden_row)
            .transpose(1, 2, 0, 3)
            .reshape(shard, owners * ways * hidden_row)
        )

    gain_row = jnp.concatenate(
        [attn_norm, attn_post_norm, ffn_norm, ffn_post_norm, query_norm, key_norm]
    )
    gain_size = gain_row.shape[0]
    attn_pack = jnp.concatenate(
        [
            jnp.concatenate(
                [lax.dynamic_slice_in_dim(w_query, part * HD, HD, 1), w_key, w_value], axis=1
            ),
            jnp.pad(gain_row[None], ((0, 15), (0, 3 * HD - gain_size))),
        ],
        axis=0,
    )
    attn_all, wo_rows, wg_all, wu_all, wd_all = gather(
        "fsdp",
        owners,
        0,
        attn_pack,
        lax.dynamic_slice_in_dim(w_output, part * out_row, out_row, 0),
        hidden_part(w_gate),
        hidden_part(w_up),
        lax.dynamic_slice_in_dim(w_down, part * hidden_row, hidden_row, 0),
    )
    gains = attn_all[:, shard, :gain_size].astype(f32)

    def gain_of(index):
        return gains[:, index * shard : (index + 1) * shard].reshape(width)

    g_attn, g_post, g_ffn, g_ffn_post = (gain_of(index) for index in range(4))
    g_query = gains[:, 4 * shard : 4 * shard + head_share].reshape(HD)
    g_key = gains[:, 4 * shard + head_share :].reshape(HD)
    w_qkv = attn_all[:, :shard].reshape(width, 3 * HD)
    wq_head, wk_full, wv_full = (w_qkv[:, i * HD : (i + 1) * HD] for i in range(3))
    wg_part = wg_all.reshape(width, owners * hidden_row)
    wu_part = wu_all.reshape(width, owners * hidden_row)
    wd_part = wd_all.reshape(owners * hidden_row, width)
    wo_head = (
        swap("ctx", ways, 1, wo_rows.reshape(ways, owners // ways * out_row, width))
        .reshape(ways, owners // ways, out_row, width)
        .transpose(1, 0, 2, 3)
        .reshape(HD, width)
    )

    attn_in = rms_gain(inputs, g_attn).astype(bf16)
    attn_seq, place_all = gather(
        "ctx", ways, 2, attn_in, jnp.broadcast_to(positions.reshape(1, rows), (8, rows))
    )
    attn_seq = attn_seq.reshape(seq, width)
    seq_place = place_all[:, 0].reshape(seq)
    index = jnp.arange(seq, dtype=jnp.int32)
    key_mask = (
        (index[None, :] <= index[:, None])
        & (index[:, None] - index[None, :] < WINDOW)
        & (index[None, :] >= (index - seq_place)[:, None])
    )
    cosine, sine_table = rope_tables(seq_place)
    cosine, sine_table = cosine[:, 0], sine_table[:, 0]
    qkv = nn(attn_seq, w_qkv)
    q_pre, k_pre, v_pre = (qkv[:, i * HD : (i + 1) * HD] for i in range(3))
    v_low = v_pre.astype(bf16)
    q_low = turned_norm(q_pre, g_query, cosine, sine_table).astype(bf16)
    k_low = turned_norm(k_pre, g_key, cosine, sine_table).astype(bf16)
    scores = jnp.where(key_mask, nt(q_low, k_low) * ATTN_SCALE, NEGATIVE)
    shifted = jnp.exp(scores - jnp.max(scores, axis=-1, keepdims=True))
    prob_rows = shifted / jnp.sum(shifted, axis=-1, keepdims=True)
    prob_low = prob_rows.astype(bf16)
    att_low = nn(prob_low, v_low).astype(bf16)

    def own_sum(key, value):
        return add_scatter(
            "ctx", ways, key, f32, value.astype(bf16).reshape(ways, rows, value.shape[1])
        )[0]

    def whole(key, value):
        return gather("ctx", ways, key, value)[0].reshape(seq, value.shape[1])

    branch = own_sum(3, nn(att_low, wo_head))
    hidden_res = inputs + rms_gain(branch, g_post)
    ffn_seq = whole(4, rms_gain(hidden_res, g_ffn).astype(bf16))
    gate_proj = nn(ffn_seq, wg_part)
    up_proj = nn(ffn_seq, wu_part)
    mixed_low = gated_gelu(gate_proj, up_proj).astype(bf16)
    down_out = own_sum(5, nn(mixed_low, wd_part))
    layer_out = hidden_res + rms_gain(down_out, g_ffn_post)

    d_down, d_ffn_post = jax.vjp(rms_gain, down_out, g_ffn_post)[1](grad_out)
    d_down_seq = whole(6, d_down.astype(bf16))
    d_mixed = nt(d_down_seq, wd_part)
    d_gate, d_up = jax.vjp(gated_gelu, gate_proj, up_proj)[1](d_mixed)
    d_gate_low = d_gate.astype(bf16)
    d_up_low = d_up.astype(bf16)
    d_ffn_in = own_sum(7, nt(d_gate_low, wg_part) + nt(d_up_low, wu_part))
    grad_w_down = tn(mixed_low, d_down_seq)
    grad_w_gate = tn(ffn_seq, d_gate_low)
    grad_w_up = tn(ffn_seq, d_up_low)
    d_hidden_part, d_ffn_norm = jax.vjp(rms_gain, hidden_res, g_ffn)[1](d_ffn_in)
    d_hidden = grad_out + d_hidden_part

    d_branch, d_post = jax.vjp(rms_gain, branch, g_post)[1](d_hidden)
    d_branch_seq = whole(8, d_branch.astype(bf16))
    grad_w_output = tn(att_low, d_branch_seq)
    d_att = nt(d_branch_seq, wo_head).astype(bf16)
    d_values = tn(prob_low, d_att)
    d_probs = nt(d_att, v_low)
    d_scores = prob_rows * (d_probs - jnp.sum(prob_rows * d_probs, axis=-1, keepdims=True))
    d_scores_low = d_scores.astype(bf16)
    d_queries = nn(d_scores_low, k_low) * ATTN_SCALE
    d_keys = tn(d_scores_low, q_low) * ATTN_SCALE
    d_q_pre, d_query_norm = jax.vjp(
        lambda values, gain_vec: turned_norm(values, gain_vec, cosine, sine_table), q_pre, g_query
    )[1](d_queries)
    dq_low = d_q_pre.astype(bf16)
    sums = own_sum(9, jnp.concatenate([nt(dq_low, wq_head), d_keys, d_values], axis=1))
    own_cos = lax.dynamic_slice_in_dim(cosine, part * rows, rows, 0)
    own_sin = lax.dynamic_slice_in_dim(sine_table, part * rows, rows, 0)
    own_k = lax.dynamic_slice_in_dim(k_pre, part * rows, rows, 0)
    d_k_pre, d_key_norm = jax.vjp(
        lambda values, gain_vec: turned_norm(values, gain_vec, own_cos, own_sin), own_k, g_key
    )[1](sums[:, width : width + HD])
    dkv_low = jnp.concatenate([d_k_pre, sums[:, width + HD :]], axis=1).astype(bf16)
    d_attn_in = sums[:, :width] + nt(dkv_low, w_qkv[:, HD:])
    dkv_seq = whole(10, dkv_low)
    d_inputs_part, d_attn_norm = jax.vjp(rms_gain, inputs, g_attn)[1](d_attn_in)
    d_tokens = d_hidden + d_inputs_part
    grad_w_query = tn(attn_seq, dq_low)
    dkv_cols = 2 * HD // ways
    grad_w_kv = tn(attn_seq, lax.dynamic_slice_in_dim(dkv_seq, part * dkv_cols, dkv_cols, 1))

    grad_wo_rows = swap(
        "ctx",
        ways,
        11,
        grad_w_output.astype(bf16)
        .reshape(owners // ways, ways, out_row, width)
        .transpose(1, 0, 2, 3)
        .reshape(ways, owners // ways * out_row, width),
    ).reshape(owners, out_row, width)
    gain_grads = jnp.concatenate(
        [
            value.reshape(owners, -1)
            for value in (d_attn_norm, d_post, d_ffn_norm, d_ffn_post, d_query_norm, d_key_norm)
        ],
        axis=1,
    )
    gain_grads = jnp.pad(gain_grads[:, None], ((0, 0), (0, 15), (0, 0)))

    def blocks(value):
        return value.astype(bf16).reshape(owners, value.shape[0] // owners, value.shape[1])

    mine = add_scatter(
        "fsdp",
        owners,
        12,
        bf16,
        blocks(grad_w_gate),
        blocks(grad_w_up),
        blocks(grad_w_down),
        blocks(grad_w_query),
        grad_wo_rows,
        blocks(grad_w_kv),
        gain_grads.astype(bf16),
    )
    wg_g, wu_g, wd_g, wq_g, wo_g, wkv_g, gain_g = gather("ctx", ways, 13, *mine)
    gain_sum = jnp.sum(gain_g[:, 0].astype(f32), axis=0)
    ends = [shard * i for i in range(1, 5)] + [4 * shard + head_share]
    t_attn, t_post, t_ffn, t_ffn_post, t_query, t_key = jnp.split(gain_sum, ends)
    half = ways // 2

    def columns(parts):
        return parts.transpose(1, 0, 2).reshape(shard, -1).astype(f32)

    return (
        layer_out.astype(bf16).reshape(1, rows, width),
        d_tokens.astype(bf16).reshape(1, rows, width),
        t_attn,
        columns(wq_g),
        columns(wkv_g[:half]),
        columns(wkv_g[half:]),
        t_query,
        t_key,
        wo_g.reshape(ways * out_row, width).astype(f32),
        t_post,
        t_ffn,
        hidden_whole(wg_g).astype(f32),
        hidden_whole(wu_g).astype(f32),
        wd_g.reshape(ways * hidden_row, width).astype(f32),
        t_ffn_post,
    )


def solution(mesh):
    return jax.shard_map(
        plain_body if mesh.shape['ctx'] != HQ or mesh.shape['fsdp'] != 2 * HQ else split_body,
        mesh=mesh,
        in_specs=(
            P("fsdp", "ctx", None),
            P("fsdp", "ctx"),
            P("fsdp", "ctx", None),
            P("fsdp"),
            P("fsdp", None),
            P("fsdp", None),
            P("fsdp", None),
            P("fsdp"),
            P("fsdp"),
            P("fsdp", None),
            P("fsdp"),
            P("fsdp"),
            P("fsdp", None),
            P("fsdp", None),
            P("fsdp", None),
            P("fsdp"),
        ),
        out_specs=(
            P("fsdp", "ctx", None),
            P("fsdp", "ctx", None),
            P("fsdp"),
            P("fsdp", None),
            P("fsdp", None),
            P("fsdp", None),
            P("fsdp"),
            P("fsdp"),
            P("fsdp", None),
            P("fsdp"),
            P("fsdp"),
            P("fsdp", None),
            P("fsdp", None),
            P("fsdp", None),
            P("fsdp"),
        ),
        check_vma=False,
    )
```

```python
import functools

import jax
import jax.numpy as jnp
from jax import lax
from jax.experimental import pallas as pl
from jax.experimental.pallas import tpu as pltpu
from jax.sharding import PartitionSpec as P

HQ = 4
HD = 256
WINDOW = 512


EPSILON = 1e-06
ATTN_SCALE = 0.0625
NEGATIVE = -1e30


def shifted_2(value, axis, steps):
    count = lax.axis_size(axis)
    leading, last = (max(0, -steps), min(count, count - steps))
    return lax.ppermute(value, axis, [(source, source + steps) for source in range(leading, last)])


def rms_gain(values, gain_vec):
    return (
        values * lax.rsqrt(jnp.mean(values * values, axis=-1, keepdims=True) + EPSILON) * gain_vec
    )


def rope_tables(seq_place):
    half_width = HD // 2
    inverse = jnp.power(10000.0, -jnp.arange(half_width, dtype=jnp.float32) * (2.0 / HD))
    angles = seq_place.astype(jnp.float32)[:, None] * inverse[None, :]
    return (jnp.cos(angles)[:, None, :], jnp.sin(angles)[:, None, :])


def rotate(values, cosine, sine_table):
    half_width = values.shape[-1] // 2
    front_half = values[..., :half_width]
    back_half = values[..., half_width:]
    return jnp.concatenate(
        [
            front_half * cosine - back_half * sine_table,
            back_half * cosine + front_half * sine_table,
        ],
        axis=-1,
    )


def query_key(q_pre, k_pre, g_query, g_key, cosine, sine_table):
    return (
        rotate(rms_gain(q_pre, g_query), cosine, sine_table),
        rotate(rms_gain(k_pre, g_key), cosine, sine_table),
    )


def gated_gelu(gate_proj, up_proj):
    return jax.nn.gelu(gate_proj, approximate=True) * up_proj


def masked_scores(q_low, key_rows, key_mask):
    raw_scores = (
        jnp.einsum("thd,kd->htk", q_low, key_rows, preferred_element_type=jnp.float32) * ATTN_SCALE
    )
    return jnp.where(key_mask[None], raw_scores, NEGATIVE)


def plain_body(
    tokens,
    positions,
    cotangent,
    attn_norm,
    w_query,
    w_key,
    w_value,
    query_norm,
    key_norm,
    w_output,
    attn_post_norm,
    ffn_norm,
    w_gate,
    w_up,
    w_down,
    ffn_post_norm,
):
    f32 = jnp.float32
    bf16 = jnp.bfloat16
    tok_rows = tokens.shape[1]
    model_width = tokens.shape[2]
    inputs = tokens.reshape(tok_rows, model_width).astype(f32)
    grad_out = cotangent.reshape(tok_rows, model_width).astype(f32)
    seq_place = positions.reshape(tok_rows)
    g_attn, wq_full, wk_full, wv_full, gq_full, gk_full, wo_full, g_attn_post = (
        lax.all_gather(attn_norm, "fsdp", axis=0, tiled=True),
        lax.all_gather(w_query, "fsdp", axis=0, tiled=True),
        lax.all_gather(w_key, "fsdp", axis=0, tiled=True),
        lax.all_gather(w_value, "fsdp", axis=0, tiled=True),
        lax.all_gather(query_norm, "fsdp", axis=0, tiled=True),
        lax.all_gather(key_norm, "fsdp", axis=0, tiled=True),
        lax.all_gather(w_output, "fsdp", axis=0, tiled=True),
        lax.all_gather(attn_post_norm, "fsdp", axis=0, tiled=True),
    )
    block_index = lax.axis_index("ctx")
    halo_count = -(-WINDOW // tok_rows)
    query_index = block_index * tok_rows + jnp.arange(tok_rows, dtype=jnp.int32)
    key_index = block_index * tok_rows + jnp.arange(
        -halo_count * tok_rows, tok_rows, dtype=jnp.int32
    )
    key_mask = (
        (key_index[None, :] <= query_index[:, None])
        & (query_index[:, None] - key_index[None, :] < WINDOW)
        & (key_index[None, :] >= (query_index - seq_place)[:, None])
    )
    attn_in = rms_gain(inputs, g_attn.astype(f32)).astype(bf16)
    q_pre = jnp.dot(attn_in, wq_full, preferred_element_type=f32).reshape(tok_rows, HQ, HD)
    k_pre = jnp.dot(attn_in, wk_full, preferred_element_type=f32).reshape(tok_rows, 1, HD)
    v_low = jnp.dot(attn_in, wv_full, preferred_element_type=f32).astype(bf16)
    cosine, sine_table = rope_tables(seq_place)
    gq_gain = gq_full.astype(f32)
    gk_gain = gk_full.astype(f32)
    q_turned, k_turned = query_key(q_pre, k_pre, gq_gain, gk_gain, cosine, sine_table)
    q_low = q_turned.astype(bf16)
    k_low = k_turned.reshape(tok_rows, HD).astype(bf16)
    key_parts = []
    value_parts = []
    for distance in range(halo_count, 0, -1):
        got_keys, got_values = shifted_2((k_low, v_low), "ctx", distance)
        key_parts.append(got_keys)
        value_parts.append(got_values)
    key_rows = jnp.concatenate(key_parts + [k_low], axis=0)
    value_rows = jnp.concatenate(value_parts + [v_low], axis=0)
    scores = masked_scores(q_low, key_rows, key_mask)
    row_max = jnp.max(scores, axis=-1, keepdims=True)
    shifted = jnp.exp(scores - row_max)
    row_total = jnp.sum(shifted, axis=-1, keepdims=True)
    log_total = row_max + jnp.log(row_total)
    prob_low = (shifted / row_total).astype(bf16)
    attended = jnp.einsum("htk,kd->thd", prob_low, value_rows, preferred_element_type=f32)
    att_low = attended.reshape(tok_rows, HQ * HD).astype(bf16)
    attn_branch = jnp.dot(att_low, wo_full, preferred_element_type=f32)
    g_post_gain = g_attn_post.astype(f32)
    hidden_res = inputs + rms_gain(attn_branch, g_post_gain)
    g_ffn, wg_full, wu_full, wd_full, g_ffn_post = (
        lax.all_gather(ffn_norm, "fsdp", axis=0, tiled=True),
        lax.all_gather(w_gate, "fsdp", axis=0, tiled=True),
        lax.all_gather(w_up, "fsdp", axis=0, tiled=True),
        lax.all_gather(w_down, "fsdp", axis=0, tiled=True),
        lax.all_gather(ffn_post_norm, "fsdp", axis=0, tiled=True),
    )
    g_ffn_gain = g_ffn.astype(f32)
    g_ffn_post_gain = g_ffn_post.astype(f32)
    ffn_in = rms_gain(hidden_res, g_ffn_gain).astype(bf16)
    gate_proj = jnp.dot(ffn_in, wg_full, preferred_element_type=f32)
    up_proj = jnp.dot(ffn_in, wu_full, preferred_element_type=f32)
    mixed_low = gated_gelu(gate_proj, up_proj).astype(bf16)
    down_out = jnp.dot(mixed_low, wd_full, preferred_element_type=f32)
    layer_out = hidden_res + rms_gain(down_out, g_ffn_post_gain)
    g_ffn, wg_full, wu_full, wd_full, g_ffn_post = (
        lax.all_gather(ffn_norm, "fsdp", axis=0, tiled=True),
        lax.all_gather(w_gate, "fsdp", axis=0, tiled=True),
        lax.all_gather(w_up, "fsdp", axis=0, tiled=True),
        lax.all_gather(w_down, "fsdp", axis=0, tiled=True),
        lax.all_gather(ffn_post_norm, "fsdp", axis=0, tiled=True),
    )
    unused, post_ffn_back = jax.vjp(rms_gain, down_out, g_ffn_post_gain)
    d_down, d_ffn_post = post_ffn_back(grad_out)
    d_down_low = d_down.astype(bf16)
    grad_w_down = jnp.einsum("tf,td->fd", mixed_low, d_down_low, preferred_element_type=f32)
    d_mixed = jnp.einsum("td,fd->tf", d_down_low, wd_full, preferred_element_type=f32)
    unused, glu_back = jax.vjp(gated_gelu, gate_proj, up_proj)
    d_gate, d_up = glu_back(d_mixed)
    d_gate_low = d_gate.astype(bf16)
    d_up_low = d_up.astype(bf16)
    grad_w_gate = jnp.einsum("td,tf->df", ffn_in, d_gate_low, preferred_element_type=f32)
    grad_w_up = jnp.einsum("td,tf->df", ffn_in, d_up_low, preferred_element_type=f32)
    d_ffn_in = jnp.einsum(
        "tf,df->td", d_gate_low, wg_full, preferred_element_type=f32
    ) + jnp.einsum("tf,df->td", d_up_low, wu_full, preferred_element_type=f32)
    unused, ffn_norm_back = jax.vjp(rms_gain, hidden_res, g_ffn_gain)
    d_hidden_part, d_ffn_norm = ffn_norm_back(d_ffn_in)
    d_hidden = grad_out + d_hidden_part
    ffn_sums = (
        lax.psum_scatter(d_ffn_norm, "fsdp", scatter_dimension=0, tiled=True),
        lax.psum_scatter(grad_w_gate, "fsdp", scatter_dimension=0, tiled=True),
        lax.psum_scatter(grad_w_up, "fsdp", scatter_dimension=0, tiled=True),
        lax.psum_scatter(grad_w_down, "fsdp", scatter_dimension=0, tiled=True),
        lax.psum_scatter(d_ffn_post, "fsdp", scatter_dimension=0, tiled=True),
    )
    g_attn, wq_full, wk_full, wv_full, gq_full, gk_full, wo_full, g_attn_post = (
        lax.all_gather(attn_norm, "fsdp", axis=0, tiled=True),
        lax.all_gather(w_query, "fsdp", axis=0, tiled=True),
        lax.all_gather(w_key, "fsdp", axis=0, tiled=True),
        lax.all_gather(w_value, "fsdp", axis=0, tiled=True),
        lax.all_gather(query_norm, "fsdp", axis=0, tiled=True),
        lax.all_gather(key_norm, "fsdp", axis=0, tiled=True),
        lax.all_gather(w_output, "fsdp", axis=0, tiled=True),
        lax.all_gather(attn_post_norm, "fsdp", axis=0, tiled=True),
    )
    unused, post_attn_back = jax.vjp(rms_gain, attn_branch, g_post_gain)
    d_branch, d_attn_post = post_attn_back(d_hidden)
    d_branch_low = d_branch.astype(bf16)
    grad_w_output = jnp.einsum("tc,td->cd", att_low, d_branch_low, preferred_element_type=f32)
    d_attended = (
        jnp.einsum("td,cd->tc", d_branch_low, wo_full, preferred_element_type=f32)
        .reshape(tok_rows, HQ, HD)
        .astype(bf16)
    )
    scores = masked_scores(q_low, key_rows, key_mask)
    prob_rows = jnp.exp(scores - log_total)
    prob_low = prob_rows.astype(bf16)
    d_values = jnp.einsum("htk,thd->kd", prob_low, d_attended, preferred_element_type=f32)
    d_probs = jnp.einsum("thd,kd->htk", d_attended, value_rows, preferred_element_type=f32)
    d_scores = prob_rows * (d_probs - jnp.sum(prob_rows * d_probs, axis=-1, keepdims=True))
    d_scores_low = d_scores.astype(bf16)
    d_queries = (
        jnp.einsum("htk,kd->thd", d_scores_low, key_rows, preferred_element_type=f32) * ATTN_SCALE
    )
    d_keys = jnp.einsum("htk,thd->kd", d_scores_low, q_low, preferred_element_type=f32) * ATTN_SCALE
    own_keys = d_keys[halo_count * tok_rows :]
    own_values = d_values[halo_count * tok_rows :]
    for distance in range(halo_count, 0, -1):
        part_index = halo_count - distance
        back_keys, back_values = shifted_2(
            (
                d_keys[part_index * tok_rows : (part_index + 1) * tok_rows],
                d_values[part_index * tok_rows : (part_index + 1) * tok_rows],
            ),
            "ctx",
            -distance,
        )
        own_keys = own_keys + back_keys
        own_values = own_values + back_values
    unused, turn_back = jax.vjp(
        lambda q_in, k_in, gq_in, gk_in: query_key(q_in, k_in, gq_in, gk_in, cosine, sine_table),
        q_pre,
        k_pre,
        gq_gain,
        gk_gain,
    )
    d_q_pre, d_k_pre, d_query_norm, d_key_norm = turn_back(
        (d_queries, own_keys.reshape(tok_rows, 1, HD))
    )
    dq_low = d_q_pre.reshape(tok_rows, HQ * HD).astype(bf16)
    dk_low = d_k_pre.reshape(tok_rows, HD).astype(bf16)
    dv_low = own_values.astype(bf16)
    grad_w_query = jnp.einsum("td,tc->dc", attn_in, dq_low, preferred_element_type=f32)
    grad_w_key = jnp.einsum("td,tc->dc", attn_in, dk_low, preferred_element_type=f32)
    grad_w_value = jnp.einsum("td,tc->dc", attn_in, dv_low, preferred_element_type=f32)
    d_attn_in = (
        jnp.einsum("tc,dc->td", dq_low, wq_full, preferred_element_type=f32)
        + jnp.einsum("tc,dc->td", dk_low, wk_full, preferred_element_type=f32)
        + jnp.einsum("tc,dc->td", dv_low, wv_full, preferred_element_type=f32)
    )
    unused, first_back = jax.vjp(rms_gain, inputs, g_attn.astype(f32))
    d_inputs_part, d_attn_norm = first_back(d_attn_in)
    d_tokens = d_hidden + d_inputs_part
    attn_sums = (
        lax.psum_scatter(d_attn_norm, "fsdp", scatter_dimension=0, tiled=True),
        lax.psum_scatter(grad_w_query, "fsdp", scatter_dimension=0, tiled=True),
        lax.psum_scatter(grad_w_key, "fsdp", scatter_dimension=0, tiled=True),
        lax.psum_scatter(grad_w_value, "fsdp", scatter_dimension=0, tiled=True),
        lax.psum_scatter(d_query_norm, "fsdp", scatter_dimension=0, tiled=True),
        lax.psum_scatter(d_key_norm, "fsdp", scatter_dimension=0, tiled=True),
        lax.psum_scatter(grad_w_output, "fsdp", scatter_dimension=0, tiled=True),
        lax.psum_scatter(d_attn_post, "fsdp", scatter_dimension=0, tiled=True),
    )
    column_sums = (
        lax.psum_scatter(attn_sums[1], "ctx", scatter_dimension=1, tiled=True),
        lax.psum_scatter(attn_sums[2], "ctx", scatter_dimension=1, tiled=True),
        lax.psum_scatter(attn_sums[3], "ctx", scatter_dimension=1, tiled=True),
        lax.psum_scatter(attn_sums[6], "ctx", scatter_dimension=1, tiled=True),
        lax.psum_scatter(ffn_sums[1], "ctx", scatter_dimension=1, tiled=True),
        lax.psum_scatter(ffn_sums[2], "ctx", scatter_dimension=1, tiled=True),
        lax.psum_scatter(ffn_sums[3], "ctx", scatter_dimension=1, tiled=True),
    )
    full_columns = (
        lax.all_gather(column_sums[0], "ctx", axis=1, tiled=True),
        lax.all_gather(column_sums[1], "ctx", axis=1, tiled=True),
        lax.all_gather(column_sums[2], "ctx", axis=1, tiled=True),
        lax.all_gather(column_sums[3], "ctx", axis=1, tiled=True),
        lax.all_gather(column_sums[4], "ctx", axis=1, tiled=True),
        lax.all_gather(column_sums[5], "ctx", axis=1, tiled=True),
        lax.all_gather(column_sums[6], "ctx", axis=1, tiled=True),
    )
    gain_totals = lax.psum(
        (attn_sums[0], attn_sums[4], attn_sums[5], attn_sums[7], ffn_sums[0], ffn_sums[4]), "ctx"
    )
    results = (
        gain_totals[0],
        full_columns[0],
        full_columns[1],
        full_columns[2],
        gain_totals[1],
        gain_totals[2],
        full_columns[3],
        gain_totals[3],
        gain_totals[4],
        full_columns[4],
        full_columns[5],
        full_columns[6],
        gain_totals[5],
    )
    out_rows = layer_out.astype(bf16).reshape(1, tok_rows, model_width)
    grad_rows = d_tokens.astype(bf16).reshape(1, tok_rows, model_width)
    return (
        out_rows,
        grad_rows,
        results[0],
        results[1],
        results[2],
        results[3],
        results[4],
        results[5],
        results[6],
        results[7],
        results[8],
        results[9],
        results[10],
        results[11],
        results[12],
    )


VMEM_BYTES = 48 * 1024 * 1024


def peer_of(axis, index):
    return dict(device_id={axis: index}, device_id_type=pl.DeviceIdType.MESH)


def greet(axis, indices):
    barrier = pltpu.get_barrier_semaphore()
    for index in indices:
        pl.semaphore_signal(barrier, inc=1, **peer_of(axis, index))
    pl.semaphore_wait(barrier, len(indices))


def gather_kernel(axis, n, count, swaps, *refs):
    every = count + swaps
    ins, outs = refs[:every], refs[every : 2 * every]
    send, recv = refs[2 * every :]
    me = lax.axis_index(axis)
    outer, inner = lax.div(me, 2), lax.rem(me, 2)
    span = n // 2
    twin = outer * 2 + (1 - inner)

    def ahead(step):
        return lax.rem(outer + step, span) * 2 + inner

    def behind(step):
        return lax.rem(outer + span - step, span)

    if swaps:
        greet(axis, [lax.rem(me + step, n) for step in range(1, n)])
    else:
        greet(axis, [twin] + [ahead(step) for step in range(1, span)])

    def trade(i, step, slot):
        target = lax.rem(me + step, n)
        return pltpu.make_async_remote_copy(
            src_ref=ins[i].at[target],
            dst_ref=outs[i].at[slot],
            send_sem=send.at[i, step - 1],
            recv_sem=recv.at[i, step - 1],
            **peer_of(axis, target),
        )

    def copy(i, source, slot, lane, target):
        return pltpu.make_async_remote_copy(
            src_ref=source,
            dst_ref=outs[i].at[slot],
            send_sem=send.at[i, lane],
            recv_sem=recv.at[i, lane],
            **peer_of(axis, target),
        )

    for i in range(count):
        for step in range(1, span):
            copy(i, ins[i], me, step, ahead(step)).start()
        copy(i, ins[i], me, 0, twin).start()
    for i in range(count, every):
        for step in range(1, n):
            trade(i, step, me).start()
    for i in range(count):
        outs[i][me] = ins[i][...]
    for i in range(count, every):
        outs[i][me] = ins[i][me]
    for i in range(count):
        for step in range(1, span):
            slot = behind(step) * 2 + inner
            copy(i, ins[i], slot, step, twin).wait_recv()
            copy(i, outs[i].at[slot], slot, span - 1 + step, twin).start()
    for i in range(count):
        copy(i, ins[i], twin, 0, twin).wait_recv()
        for step in range(1, span):
            slot = behind(step) * 2 + (1 - inner)
            copy(i, ins[i], slot, span - 1 + step, twin).wait_recv()
        for lane in range(2 * span - 1):
            copy(i, ins[i], me, lane, twin).wait_send()
    for i in range(count, every):
        for step in range(1, n):
            trade(i, step, lax.rem(me + n - step, n)).wait_recv()
        for step in range(1, n):
            trade(i, step, me).wait_send()


def gather(axis, n, key, *arrays, swapped=()):
    kept = len(arrays)
    shapes = [(n,) + a.shape for a in arrays] + [a.shape for a in swapped]
    arrays = arrays + swapped
    count = len(arrays)
    spec = pl.BlockSpec(memory_space=pltpu.VMEM)
    return pl.pallas_call(
        functools.partial(gather_kernel, axis, n, kept, len(swapped)),
        out_shape=[jax.ShapeDtypeStruct(shape, a.dtype) for shape, a in zip(shapes, arrays)],
        in_specs=[spec] * count,
        out_specs=[spec] * count,
        scratch_shapes=[
            pltpu.SemaphoreType.DMA((count, n - 1)),
            pltpu.SemaphoreType.DMA((count, n - 1)),
        ],
        compiler_params=pltpu.CompilerParams(
            collective_id=key, has_side_effects=True, vmem_limit_bytes=VMEM_BYTES
        ),
    )(*arrays)


def add_scatter_kernel(axis, n, count, *refs):
    ins, outs = refs[:count], refs[count : 2 * count]
    from_twin, paired, landed = (
        refs[2 * count : 3 * count],
        refs[3 * count : 4 * count],
        refs[4 * count : 5 * count],
    )
    send, recv = refs[5 * count :]
    me = lax.axis_index(axis)
    outer, inner = lax.div(me, 2), lax.rem(me, 2)
    span = n // 2
    twin = outer * 2 + (1 - inner)
    f32 = jnp.float32

    def ahead(step):
        return lax.rem(outer + step, span)

    greet(axis, [twin] + [ahead(step) * 2 + inner for step in range(1, span)])

    def to_twin(i, step):
        return pltpu.make_async_remote_copy(
            src_ref=ins[i].at[ahead(step) * 2 + (1 - inner)],
            dst_ref=from_twin[i].at[step],
            send_sem=send.at[i, step],
            recv_sem=recv.at[i, step],
            **peer_of(axis, twin),
        )

    def to_owner(i, step):
        return pltpu.make_async_remote_copy(
            src_ref=paired[i].at[step],
            dst_ref=landed[i].at[step],
            send_sem=send.at[i, span + step],
            recv_sem=recv.at[i, span + step],
            **peer_of(axis, ahead(step) * 2 + inner),
        )

    order = list(range(1, span)) + [0]
    for i in range(count):
        for step in order:
            to_twin(i, step).start()
    for i in range(count):
        for step in range(1, span):
            to_twin(i, step).wait_recv()
            paired[i][step] = (
                ins[i][ahead(step) * 2 + inner].astype(f32) + from_twin[i][step].astype(f32)
            ).astype(paired[i].dtype)
            to_owner(i, step).start()
    for i in range(count):
        to_twin(i, 0).wait_recv()
        total = ins[i][me].astype(f32) + from_twin[i][0].astype(f32)
        for step in range(1, span):
            to_owner(i, step).wait_recv()
            total = total + landed[i][step].astype(f32)
        outs[i][...] = total.astype(outs[i].dtype)
    for i in range(count):
        for step in range(span):
            to_twin(i, step).wait_send()
        for step in range(1, span):
            to_owner(i, step).wait_send()


def add_scatter(axis, n, key, out_type, *arrays):
    count = len(arrays)
    spec = pl.BlockSpec(memory_space=pltpu.VMEM)
    slots = [pltpu.VMEM((n // 2,) + a.shape[1:], a.dtype) for a in arrays]
    return pl.pallas_call(
        functools.partial(add_scatter_kernel, axis, n, count),
        out_shape=[jax.ShapeDtypeStruct(a.shape[1:], out_type) for a in arrays],
        in_specs=[spec] * count,
        out_specs=[spec] * count,
        scratch_shapes=slots * 3
        + [
            pltpu.SemaphoreType.DMA((count, n)),
            pltpu.SemaphoreType.DMA((count, n)),
        ],
        compiler_params=pltpu.CompilerParams(
            collective_id=key, has_side_effects=True, vmem_limit_bytes=VMEM_BYTES
        ),
    )(*arrays)


def finish_kernel(owners, ways, sums, count, *refs):
    ins, outs = refs[:count], refs[count : 2 * count]
    refs = refs[2 * count :]
    from_twin, paired, landed = refs[:sums], refs[sums : 2 * sums], refs[2 * sums : 3 * sums]
    send, recv, send_ctx, recv_ctx = refs[3 * sums :]
    f32 = jnp.float32
    me = lax.axis_index("fsdp")
    outer, inner = lax.div(me, 2), lax.rem(me, 2)
    span = owners // 2
    twin = outer * 2 + (1 - inner)
    part = lax.axis_index("ctx")
    side, core = lax.div(part, 2), lax.rem(part, 2)
    reach = ways // 2
    mate = side * 2 + (1 - core)

    def ahead(step):
        return lax.rem(outer + step, span)

    def across(step):
        return lax.rem(side + step, reach) * 2 + core

    def behind(step):
        return lax.rem(side + reach - step, reach)

    barrier = pltpu.get_barrier_semaphore()
    fsdp_peers = [twin] + [ahead(step) * 2 + inner for step in range(1, span)]
    ctx_peers = [mate] + [across(step) for step in range(1, reach)]
    for index in fsdp_peers:
        pl.semaphore_signal(barrier, inc=1, **peer_of("fsdp", index))
    for index in ctx_peers:
        pl.semaphore_signal(barrier, inc=1, **peer_of("ctx", index))
    pl.semaphore_wait(barrier, len(fsdp_peers) + len(ctx_peers))

    def to_twin(i, step):
        return pltpu.make_async_remote_copy(
            src_ref=ins[i].at[ahead(step) * 2 + (1 - inner)],
            dst_ref=from_twin[i].at[step],
            send_sem=send.at[i, step],
            recv_sem=recv.at[i, step],
            **peer_of("fsdp", twin),
        )

    def to_owner(i, step):
        return pltpu.make_async_remote_copy(
            src_ref=paired[i].at[step],
            dst_ref=landed[i].at[step],
            send_sem=send.at[i, span + step],
            recv_sem=recv.at[i, span + step],
            **peer_of("fsdp", ahead(step) * 2 + inner),
        )

    def spread(i, slot, lane, target):
        return pltpu.make_async_remote_copy(
            src_ref=outs[i].at[slot],
            dst_ref=outs[i].at[slot],
            send_sem=send_ctx.at[i, lane],
            recv_sem=recv_ctx.at[i, lane],
            **peer_of("ctx", target),
        )

    def publish(i):
        for step in range(1, reach):
            spread(i, part, step, across(step)).start()
        spread(i, part, 0, mate).start()

    for i in range(sums):
        for step in list(range(1, span)) + [0]:
            to_twin(i, step).start()
    for i in range(sums, count):
        outs[i][part] = ins[i][...]
        publish(i)
    for i in range(sums):
        for step in range(1, span):
            to_twin(i, step).wait_recv()
            paired[i][step] = (
                ins[i][ahead(step) * 2 + inner].astype(f32) + from_twin[i][step].astype(f32)
            ).astype(paired[i].dtype)
            to_owner(i, step).start()
    for i in range(sums):
        to_twin(i, 0).wait_recv()
        total = ins[i][me].astype(f32) + from_twin[i][0].astype(f32)
        for step in range(1, span):
            to_owner(i, step).wait_recv()
            total = total + landed[i][step].astype(f32)
        outs[i][part] = total.astype(outs[i].dtype)
        publish(i)
    turn = list(range(sums, count)) + list(range(sums))
    for i in turn:
        for step in range(1, reach):
            slot = behind(step) * 2 + core
            spread(i, slot, step, mate).wait_recv()
            spread(i, slot, reach - 1 + step, mate).start()
    for i in turn:
        spread(i, mate, 0, mate).wait_recv()
        for step in range(1, reach):
            spread(i, behind(step) * 2 + (1 - core), reach - 1 + step, mate).wait_recv()
        for lane in range(2 * reach - 1):
            spread(i, part, lane, mate).wait_send()
    for i in range(sums):
        for step in range(span):
            to_twin(i, step).wait_send()
        for step in range(1, span):
            to_owner(i, step).wait_send()


def finish(owners, ways, key, summed, others):
    arrays = summed + others
    sums, count = len(summed), len(arrays)
    spec = pl.BlockSpec(memory_space=pltpu.VMEM)
    shapes = [(ways,) + a.shape[1:] for a in summed] + [(ways,) + a.shape for a in others]
    slots = [pltpu.VMEM((owners // 2,) + a.shape[1:], a.dtype) for a in summed]
    return pl.pallas_call(
        functools.partial(finish_kernel, owners, ways, sums, count),
        out_shape=[jax.ShapeDtypeStruct(shape, a.dtype) for shape, a in zip(shapes, arrays)],
        in_specs=[spec] * count,
        out_specs=[spec] * count,
        scratch_shapes=slots * 3
        + [pltpu.SemaphoreType.DMA((sums, owners))] * 2
        + [pltpu.SemaphoreType.DMA((count, ways - 1))] * 2,
        compiler_params=pltpu.CompilerParams(
            collective_id=key, has_side_effects=True, vmem_limit_bytes=VMEM_BYTES
        ),
    )(*arrays)


def turned_norm(values, gain_vec, cosine, sine_table):
    return rotate(rms_gain(values, gain_vec), cosine, sine_table)


def split_body(
    tokens,
    positions,
    cotangent,
    attn_norm,
    w_query,
    w_key,
    w_value,
    query_norm,
    key_norm,
    w_output,
    attn_post_norm,
    ffn_norm,
    w_gate,
    w_up,
    w_down,
    ffn_post_norm,
):
    f32 = jnp.float32
    bf16 = jnp.bfloat16
    ways = lax.axis_size("ctx")
    owners = lax.axis_size("fsdp")
    part = lax.axis_index("ctx")
    rows, width = tokens.shape[1:]
    seq = rows * ways
    shard = w_query.shape[0]
    hidden_row = w_down.shape[0] // ways
    out_row = w_output.shape[0] // ways
    head_share = query_norm.shape[0]
    inputs = tokens.reshape(rows, width).astype(f32)
    grad_out = cotangent.reshape(rows, width).astype(f32)

    def mul(left, right, dims):
        return lax.dot_general(left, right, (dims, ((), ())), preferred_element_type=f32)

    def nn(left, right):
        return mul(left, right, ((1,), (0,)))

    def nt(left, right):
        return mul(left, right, ((1,), (1,)))

    def tn(left, right):
        return mul(left, right, ((0,), (0,)))

    def hidden_part(weight):
        cut = weight.reshape(shard, owners, ways, hidden_row)
        return lax.dynamic_index_in_dim(cut, part, 2, keepdims=False).reshape(
            shard, owners * hidden_row
        )

    def hidden_whole(parts):
        return (
            parts.reshape(ways, shard, owners, hidden_row)
            .transpose(1, 2, 0, 3)
            .reshape(shard, owners * ways * hidden_row)
        )

    gain_row = jnp.concatenate(
        [attn_norm, attn_post_norm, ffn_norm, ffn_post_norm, query_norm, key_norm]
    )
    gain_size = gain_row.shape[0]
    attn_pack = jnp.concatenate(
        [
            jnp.concatenate(
                [lax.dynamic_slice_in_dim(w_query, part * HD, HD, 1), w_key, w_value], axis=1
            ),
            jnp.pad(gain_row[None], ((0, 15), (0, 3 * HD - gain_size))),
        ],
        axis=0,
    )
    hidden_cols = owners * hidden_row
    wgu_part = lax.all_gather(
        jnp.concatenate([hidden_part(w_gate), hidden_part(w_up)], axis=1),
        "fsdp",
        axis=0,
        tiled=True,
    )
    wd_part = lax.all_gather(
        lax.dynamic_slice_in_dim(w_down, part * hidden_row, hidden_row, 0),
        "fsdp",
        axis=0,
        tiled=True,
    )
    attn_all, wo_rows = gather(
        "fsdp",
        owners,
        0,
        attn_pack,
        lax.dynamic_slice_in_dim(w_output, part * out_row, out_row, 0),
    )
    gains = attn_all[:, shard, :gain_size].astype(f32)

    def gain_of(index):
        return gains[:, index * shard : (index + 1) * shard].reshape(width)

    g_attn, g_post, g_ffn, g_ffn_post = (gain_of(index) for index in range(4))
    g_query = gains[:, 4 * shard : 4 * shard + head_share].reshape(HD)
    g_key = gains[:, 4 * shard + head_share :].reshape(HD)
    w_qkv = attn_all[:, :shard].reshape(width, 3 * HD)
    wq_head, wk_full, wv_full = (w_qkv[:, i * HD : (i + 1) * HD] for i in range(3))
    attn_in = rms_gain(inputs, g_attn).astype(bf16)
    attn_seq, place_all, wo_head = gather(
        "ctx",
        ways,
        2,
        attn_in,
        jnp.broadcast_to(positions.reshape(1, rows), (8, rows)),
        swapped=(wo_rows.reshape(ways, owners // ways * out_row, width),),
    )
    wo_head = (
        wo_head.reshape(ways, owners // ways, out_row, width)
        .transpose(1, 0, 2, 3)
        .reshape(HD, width)
    )
    attn_seq = attn_seq.reshape(seq, width)
    seq_place = place_all[:, 0].reshape(seq)
    index = jnp.arange(seq, dtype=jnp.int32)
    key_mask = (
        (index[None, :] <= index[:, None])
        & (index[:, None] - index[None, :] < WINDOW)
        & (index[None, :] >= (index - seq_place)[:, None])
    )
    cosine, sine_table = rope_tables(seq_place)
    cosine, sine_table = cosine[:, 0], sine_table[:, 0]
    qkv = nn(attn_seq, w_qkv)
    q_pre, k_pre, v_pre = (qkv[:, i * HD : (i + 1) * HD] for i in range(3))
    v_low = v_pre.astype(bf16)
    q_low = turned_norm(q_pre, g_query, cosine, sine_table).astype(bf16)
    k_low = turned_norm(k_pre, g_key, cosine, sine_table).astype(bf16)
    scores = jnp.where(key_mask, nt(q_low, k_low) * ATTN_SCALE, NEGATIVE)
    shifted = jnp.exp(scores - jnp.max(scores, axis=-1, keepdims=True))
    prob_rows = shifted / jnp.sum(shifted, axis=-1, keepdims=True)
    prob_low = prob_rows.astype(bf16)
    att_low = nn(prob_low, v_low).astype(bf16)

    def own_sum(key, value):
        return add_scatter(
            "ctx", ways, key, f32, value.astype(bf16).reshape(ways, rows, value.shape[1])
        )[0]

    def whole(key, value):
        return gather("ctx", ways, key, value)[0].reshape(seq, value.shape[1])

    branch = own_sum(3, nn(att_low, wo_head))
    hidden_res = inputs + rms_gain(branch, g_post)
    ffn_seq = whole(4, rms_gain(hidden_res, g_ffn).astype(bf16))
    gate_up = nn(ffn_seq, wgu_part)
    gate_proj, up_proj = gate_up[:, :hidden_cols], gate_up[:, hidden_cols:]
    mixed_low = gated_gelu(gate_proj, up_proj).astype(bf16)
    down_out = own_sum(5, nn(mixed_low, wd_part))
    layer_out = hidden_res + rms_gain(down_out, g_ffn_post)

    d_down, d_ffn_post = jax.vjp(rms_gain, down_out, g_ffn_post)[1](grad_out)
    d_down_seq = whole(6, d_down.astype(bf16))
    d_mixed = nt(d_down_seq, wd_part)
    d_gate, d_up = jax.vjp(gated_gelu, gate_proj, up_proj)[1](d_mixed)
    d_gate_up = jnp.concatenate([d_gate.astype(bf16), d_up.astype(bf16)], axis=1)
    d_ffn_in = own_sum(7, nt(d_gate_up, wgu_part))
    wd_g = lax.psum_scatter(
        tn(mixed_low, d_down_seq).astype(bf16), "fsdp", scatter_dimension=0, tiled=True
    )
    wgu_g = lax.psum_scatter(
        tn(ffn_seq, d_gate_up).astype(bf16), "fsdp", scatter_dimension=0, tiled=True
    )
    d_hidden_part, d_ffn_norm = jax.vjp(rms_gain, hidden_res, g_ffn)[1](d_ffn_in)
    d_hidden = grad_out + d_hidden_part

    d_branch, d_post = jax.vjp(rms_gain, branch, g_post)[1](d_hidden)
    d_branch_seq = whole(8, d_branch.astype(bf16))
    grad_w_output = tn(att_low, d_branch_seq)
    d_att = nt(d_branch_seq, wo_head).astype(bf16)
    d_values = tn(prob_low, d_att)
    d_probs = nt(d_att, v_low)
    d_scores = prob_rows * (d_probs - jnp.sum(prob_rows * d_probs, axis=-1, keepdims=True))
    d_scores_low = d_scores.astype(bf16)
    d_queries = nn(d_scores_low, k_low) * ATTN_SCALE
    d_keys = tn(d_scores_low, q_low) * ATTN_SCALE
    d_q_pre, d_query_norm = jax.vjp(
        lambda values, gain_vec: turned_norm(values, gain_vec, cosine, sine_table), q_pre, g_query
    )[1](d_queries)
    dq_low = d_q_pre.astype(bf16)
    sums = own_sum(9, jnp.concatenate([nt(dq_low, wq_head), d_keys, d_values], axis=1))
    own_cos = lax.dynamic_slice_in_dim(cosine, part * rows, rows, 0)
    own_sin = lax.dynamic_slice_in_dim(sine_table, part * rows, rows, 0)
    own_k = lax.dynamic_slice_in_dim(k_pre, part * rows, rows, 0)
    d_k_pre, d_key_norm = jax.vjp(
        lambda values, gain_vec: turned_norm(values, gain_vec, own_cos, own_sin), own_k, g_key
    )[1](sums[:, width : width + HD])
    dkv_low = jnp.concatenate([d_k_pre, sums[:, width + HD :]], axis=1).astype(bf16)
    d_attn_in = sums[:, :width] + nt(dkv_low, w_qkv[:, HD:])
    dkv_seq, grad_wo_rows = gather(
        "ctx",
        ways,
        10,
        dkv_low,
        swapped=(
            grad_w_output.astype(bf16)
            .reshape(owners // ways, ways, out_row, width)
            .transpose(1, 0, 2, 3)
            .reshape(ways, owners // ways * out_row, width),
        ),
    )
    dkv_seq = dkv_seq.reshape(seq, 2 * HD)
    grad_wo_rows = grad_wo_rows.reshape(owners, out_row, width)
    d_inputs_part, d_attn_norm = jax.vjp(rms_gain, inputs, g_attn)[1](d_attn_in)
    d_tokens = d_hidden + d_inputs_part
    grad_w_query = tn(attn_seq, dq_low)
    dkv_cols = 2 * HD // ways
    grad_w_kv = tn(attn_seq, lax.dynamic_slice_in_dim(dkv_seq, part * dkv_cols, dkv_cols, 1))

    gain_grads = jnp.concatenate(
        [
            value.reshape(owners, -1)
            for value in (d_attn_norm, d_post, d_ffn_norm, d_ffn_post, d_query_norm, d_key_norm)
        ],
        axis=1,
    )
    gain_grads = jnp.pad(gain_grads[:, None], ((0, 0), (0, 15), (0, 0)))

    def blocks(value):
        return value.astype(bf16).reshape(owners, value.shape[0] // owners, value.shape[1])

    wq_g, wo_g, wkv_g, gain_g, wgu_g, wd_g = finish(
        owners,
        ways,
        12,
        [blocks(grad_w_query), grad_wo_rows, blocks(grad_w_kv), gain_grads.astype(bf16)],
        [wgu_g, wd_g],
    )
    gain_sum = jnp.sum(gain_g[:, 0].astype(f32), axis=0)
    ends = [shard * i for i in range(1, 5)] + [4 * shard + head_share]
    t_attn, t_post, t_ffn, t_ffn_post, t_query, t_key = jnp.split(gain_sum, ends)
    half = ways // 2

    def columns(parts):
        return parts.transpose(1, 0, 2).reshape(shard, -1).astype(f32)

    return (
        layer_out.astype(bf16).reshape(1, rows, width),
        d_tokens.astype(bf16).reshape(1, rows, width),
        t_attn,
        columns(wq_g),
        columns(wkv_g[:half]),
        columns(wkv_g[half:]),
        t_query,
        t_key,
        wo_g.reshape(ways * out_row, width).astype(f32),
        t_post,
        t_ffn,
        hidden_whole(wgu_g[:, :, :hidden_cols]).astype(f32),
        hidden_whole(wgu_g[:, :, hidden_cols:]).astype(f32),
        wd_g.reshape(ways * hidden_row, width).astype(f32),
        t_ffn_post,
    )


def solution(mesh):
    return jax.shard_map(
        plain_body if mesh.shape['ctx'] != HQ or mesh.shape['fsdp'] != 2 * HQ else split_body,
        mesh=mesh,
        in_specs=(
            P("fsdp", "ctx", None),
            P("fsdp", "ctx"),
            P("fsdp", "ctx", None),
            P("fsdp"),
            P("fsdp", None),
            P("fsdp", None),
            P("fsdp", None),
            P("fsdp"),
            P("fsdp"),
            P("fsdp", None),
            P("fsdp"),
            P("fsdp"),
            P("fsdp", None),
            P("fsdp", None),
            P("fsdp", None),
            P("fsdp"),
        ),
        out_specs=(
            P("fsdp", "ctx", None),
            P("fsdp", "ctx", None),
            P("fsdp"),
            P("fsdp", None),
            P("fsdp", None),
            P("fsdp", None),
            P("fsdp"),
            P("fsdp"),
            P("fsdp", None),
            P("fsdp"),
            P("fsdp"),
            P("fsdp", None),
            P("fsdp", None),
            P("fsdp", None),
            P("fsdp"),
        ),
        check_vma=False,
    )
```

```python
import functools

import jax
import jax.numpy as jnp
from jax import lax
from jax.experimental import pallas as pl
from jax.experimental.pallas import tpu as pltpu
from jax.sharding import PartitionSpec as P

HQ = 4
HD = 256
WINDOW = 512


EPSILON = 1e-06
ATTN_SCALE = 0.0625
NEGATIVE = -1e30


def shifted_2(value, axis, steps):
    count = lax.axis_size(axis)
    leading, last = (max(0, -steps), min(count, count - steps))
    return lax.ppermute(value, axis, [(source, source + steps) for source in range(leading, last)])


def rms_gain(values, gain_vec):
    return (
        values * lax.rsqrt(jnp.mean(values * values, axis=-1, keepdims=True) + EPSILON) * gain_vec
    )


def rope_tables(seq_place):
    half_width = HD // 2
    inverse = jnp.power(10000.0, -jnp.arange(half_width, dtype=jnp.float32) * (2.0 / HD))
    angles = seq_place.astype(jnp.float32)[:, None] * inverse[None, :]
    return (jnp.cos(angles)[:, None, :], jnp.sin(angles)[:, None, :])


def rotate(values, cosine, sine_table):
    half_width = values.shape[-1] // 2
    front_half = values[..., :half_width]
    back_half = values[..., half_width:]
    return jnp.concatenate(
        [
            front_half * cosine - back_half * sine_table,
            back_half * cosine + front_half * sine_table,
        ],
        axis=-1,
    )


def query_key(q_pre, k_pre, g_query, g_key, cosine, sine_table):
    return (
        rotate(rms_gain(q_pre, g_query), cosine, sine_table),
        rotate(rms_gain(k_pre, g_key), cosine, sine_table),
    )


def gated_gelu(gate_proj, up_proj):
    return jax.nn.gelu(gate_proj, approximate=True) * up_proj


def masked_scores(q_low, key_rows, key_mask):
    raw_scores = (
        jnp.einsum("thd,kd->htk", q_low, key_rows, preferred_element_type=jnp.float32) * ATTN_SCALE
    )
    return jnp.where(key_mask[None], raw_scores, NEGATIVE)


def plain_body(
    tokens,
    positions,
    cotangent,
    attn_norm,
    w_query,
    w_key,
    w_value,
    query_norm,
    key_norm,
    w_output,
    attn_post_norm,
    ffn_norm,
    w_gate,
    w_up,
    w_down,
    ffn_post_norm,
):
    f32 = jnp.float32
    bf16 = jnp.bfloat16
    tok_rows = tokens.shape[1]
    model_width = tokens.shape[2]
    inputs = tokens.reshape(tok_rows, model_width).astype(f32)
    grad_out = cotangent.reshape(tok_rows, model_width).astype(f32)
    seq_place = positions.reshape(tok_rows)
    g_attn, wq_full, wk_full, wv_full, gq_full, gk_full, wo_full, g_attn_post = (
        lax.all_gather(attn_norm, "fsdp", axis=0, tiled=True),
        lax.all_gather(w_query, "fsdp", axis=0, tiled=True),
        lax.all_gather(w_key, "fsdp", axis=0, tiled=True),
        lax.all_gather(w_value, "fsdp", axis=0, tiled=True),
        lax.all_gather(query_norm, "fsdp", axis=0, tiled=True),
        lax.all_gather(key_norm, "fsdp", axis=0, tiled=True),
        lax.all_gather(w_output, "fsdp", axis=0, tiled=True),
        lax.all_gather(attn_post_norm, "fsdp", axis=0, tiled=True),
    )
    block_index = lax.axis_index("ctx")
    halo_count = -(-WINDOW // tok_rows)
    query_index = block_index * tok_rows + jnp.arange(tok_rows, dtype=jnp.int32)
    key_index = block_index * tok_rows + jnp.arange(
        -halo_count * tok_rows, tok_rows, dtype=jnp.int32
    )
    key_mask = (
        (key_index[None, :] <= query_index[:, None])
        & (query_index[:, None] - key_index[None, :] < WINDOW)
        & (key_index[None, :] >= (query_index - seq_place)[:, None])
    )
    attn_in = rms_gain(inputs, g_attn.astype(f32)).astype(bf16)
    q_pre = jnp.dot(attn_in, wq_full, preferred_element_type=f32).reshape(tok_rows, HQ, HD)
    k_pre = jnp.dot(attn_in, wk_full, preferred_element_type=f32).reshape(tok_rows, 1, HD)
    v_low = jnp.dot(attn_in, wv_full, preferred_element_type=f32).astype(bf16)
    cosine, sine_table = rope_tables(seq_place)
    gq_gain = gq_full.astype(f32)
    gk_gain = gk_full.astype(f32)
    q_turned, k_turned = query_key(q_pre, k_pre, gq_gain, gk_gain, cosine, sine_table)
    q_low = q_turned.astype(bf16)
    k_low = k_turned.reshape(tok_rows, HD).astype(bf16)
    key_parts = []
    value_parts = []
    for distance in range(halo_count, 0, -1):
        got_keys, got_values = shifted_2((k_low, v_low), "ctx", distance)
        key_parts.append(got_keys)
        value_parts.append(got_values)
    key_rows = jnp.concatenate(key_parts + [k_low], axis=0)
    value_rows = jnp.concatenate(value_parts + [v_low], axis=0)
    scores = masked_scores(q_low, key_rows, key_mask)
    row_max = jnp.max(scores, axis=-1, keepdims=True)
    shifted = jnp.exp(scores - row_max)
    row_total = jnp.sum(shifted, axis=-1, keepdims=True)
    log_total = row_max + jnp.log(row_total)
    prob_low = (shifted / row_total).astype(bf16)
    attended = jnp.einsum("htk,kd->thd", prob_low, value_rows, preferred_element_type=f32)
    att_low = attended.reshape(tok_rows, HQ * HD).astype(bf16)
    attn_branch = jnp.dot(att_low, wo_full, preferred_element_type=f32)
    g_post_gain = g_attn_post.astype(f32)
    hidden_res = inputs + rms_gain(attn_branch, g_post_gain)
    g_ffn, wg_full, wu_full, wd_full, g_ffn_post = (
        lax.all_gather(ffn_norm, "fsdp", axis=0, tiled=True),
        lax.all_gather(w_gate, "fsdp", axis=0, tiled=True),
        lax.all_gather(w_up, "fsdp", axis=0, tiled=True),
        lax.all_gather(w_down, "fsdp", axis=0, tiled=True),
        lax.all_gather(ffn_post_norm, "fsdp", axis=0, tiled=True),
    )
    g_ffn_gain = g_ffn.astype(f32)
    g_ffn_post_gain = g_ffn_post.astype(f32)
    ffn_in = rms_gain(hidden_res, g_ffn_gain).astype(bf16)
    gate_proj = jnp.dot(ffn_in, wg_full, preferred_element_type=f32)
    up_proj = jnp.dot(ffn_in, wu_full, preferred_element_type=f32)
    mixed_low = gated_gelu(gate_proj, up_proj).astype(bf16)
    down_out = jnp.dot(mixed_low, wd_full, preferred_element_type=f32)
    layer_out = hidden_res + rms_gain(down_out, g_ffn_post_gain)
    g_ffn, wg_full, wu_full, wd_full, g_ffn_post = (
        lax.all_gather(ffn_norm, "fsdp", axis=0, tiled=True),
        lax.all_gather(w_gate, "fsdp", axis=0, tiled=True),
        lax.all_gather(w_up, "fsdp", axis=0, tiled=True),
        lax.all_gather(w_down, "fsdp", axis=0, tiled=True),
        lax.all_gather(ffn_post_norm, "fsdp", axis=0, tiled=True),
    )
    unused, post_ffn_back = jax.vjp(rms_gain, down_out, g_ffn_post_gain)
    d_down, d_ffn_post = post_ffn_back(grad_out)
    d_down_low = d_down.astype(bf16)
    grad_w_down = jnp.einsum("tf,td->fd", mixed_low, d_down_low, preferred_element_type=f32)
    d_mixed = jnp.einsum("td,fd->tf", d_down_low, wd_full, preferred_element_type=f32)
    unused, glu_back = jax.vjp(gated_gelu, gate_proj, up_proj)
    d_gate, d_up = glu_back(d_mixed)
    d_gate_low = d_gate.astype(bf16)
    d_up_low = d_up.astype(bf16)
    grad_w_gate = jnp.einsum("td,tf->df", ffn_in, d_gate_low, preferred_element_type=f32)
    grad_w_up = jnp.einsum("td,tf->df", ffn_in, d_up_low, preferred_element_type=f32)
    d_ffn_in = jnp.einsum(
        "tf,df->td", d_gate_low, wg_full, preferred_element_type=f32
    ) + jnp.einsum("tf,df->td", d_up_low, wu_full, preferred_element_type=f32)
    unused, ffn_norm_back = jax.vjp(rms_gain, hidden_res, g_ffn_gain)
    d_hidden_part, d_ffn_norm = ffn_norm_back(d_ffn_in)
    d_hidden = grad_out + d_hidden_part
    ffn_sums = (
        lax.psum_scatter(d_ffn_norm, "fsdp", scatter_dimension=0, tiled=True),
        lax.psum_scatter(grad_w_gate, "fsdp", scatter_dimension=0, tiled=True),
        lax.psum_scatter(grad_w_up, "fsdp", scatter_dimension=0, tiled=True),
        lax.psum_scatter(grad_w_down, "fsdp", scatter_dimension=0, tiled=True),
        lax.psum_scatter(d_ffn_post, "fsdp", scatter_dimension=0, tiled=True),
    )
    g_attn, wq_full, wk_full, wv_full, gq_full, gk_full, wo_full, g_attn_post = (
        lax.all_gather(attn_norm, "fsdp", axis=0, tiled=True),
        lax.all_gather(w_query, "fsdp", axis=0, tiled=True),
        lax.all_gather(w_key, "fsdp", axis=0, tiled=True),
        lax.all_gather(w_value, "fsdp", axis=0, tiled=True),
        lax.all_gather(query_norm, "fsdp", axis=0, tiled=True),
        lax.all_gather(key_norm, "fsdp", axis=0, tiled=True),
        lax.all_gather(w_output, "fsdp", axis=0, tiled=True),
        lax.all_gather(attn_post_norm, "fsdp", axis=0, tiled=True),
    )
    unused, post_attn_back = jax.vjp(rms_gain, attn_branch, g_post_gain)
    d_branch, d_attn_post = post_attn_back(d_hidden)
    d_branch_low = d_branch.astype(bf16)
    grad_w_output = jnp.einsum("tc,td->cd", att_low, d_branch_low, preferred_element_type=f32)
    d_attended = (
        jnp.einsum("td,cd->tc", d_branch_low, wo_full, preferred_element_type=f32)
        .reshape(tok_rows, HQ, HD)
        .astype(bf16)
    )
    scores = masked_scores(q_low, key_rows, key_mask)
    prob_rows = jnp.exp(scores - log_total)
    prob_low = prob_rows.astype(bf16)
    d_values = jnp.einsum("htk,thd->kd", prob_low, d_attended, preferred_element_type=f32)
    d_probs = jnp.einsum("thd,kd->htk", d_attended, value_rows, preferred_element_type=f32)
    d_scores = prob_rows * (d_probs - jnp.sum(prob_rows * d_probs, axis=-1, keepdims=True))
    d_scores_low = d_scores.astype(bf16)
    d_queries = (
        jnp.einsum("htk,kd->thd", d_scores_low, key_rows, preferred_element_type=f32) * ATTN_SCALE
    )
    d_keys = jnp.einsum("htk,thd->kd", d_scores_low, q_low, preferred_element_type=f32) * ATTN_SCALE
    own_keys = d_keys[halo_count * tok_rows :]
    own_values = d_values[halo_count * tok_rows :]
    for distance in range(halo_count, 0, -1):
        part_index = halo_count - distance
        back_keys, back_values = shifted_2(
            (
                d_keys[part_index * tok_rows : (part_index + 1) * tok_rows],
                d_values[part_index * tok_rows : (part_index + 1) * tok_rows],
            ),
            "ctx",
            -distance,
        )
        own_keys = own_keys + back_keys
        own_values = own_values + back_values
    unused, turn_back = jax.vjp(
        lambda q_in, k_in, gq_in, gk_in: query_key(q_in, k_in, gq_in, gk_in, cosine, sine_table),
        q_pre,
        k_pre,
        gq_gain,
        gk_gain,
    )
    d_q_pre, d_k_pre, d_query_norm, d_key_norm = turn_back(
        (d_queries, own_keys.reshape(tok_rows, 1, HD))
    )
    dq_low = d_q_pre.reshape(tok_rows, HQ * HD).astype(bf16)
    dk_low = d_k_pre.reshape(tok_rows, HD).astype(bf16)
    dv_low = own_values.astype(bf16)
    grad_w_query = jnp.einsum("td,tc->dc", attn_in, dq_low, preferred_element_type=f32)
    grad_w_key = jnp.einsum("td,tc->dc", attn_in, dk_low, preferred_element_type=f32)
    grad_w_value = jnp.einsum("td,tc->dc", attn_in, dv_low, preferred_element_type=f32)
    d_attn_in = (
        jnp.einsum("tc,dc->td", dq_low, wq_full, preferred_element_type=f32)
        + jnp.einsum("tc,dc->td", dk_low, wk_full, preferred_element_type=f32)
        + jnp.einsum("tc,dc->td", dv_low, wv_full, preferred_element_type=f32)
    )
    unused, first_back = jax.vjp(rms_gain, inputs, g_attn.astype(f32))
    d_inputs_part, d_attn_norm = first_back(d_attn_in)
    d_tokens = d_hidden + d_inputs_part
    attn_sums = (
        lax.psum_scatter(d_attn_norm, "fsdp", scatter_dimension=0, tiled=True),
        lax.psum_scatter(grad_w_query, "fsdp", scatter_dimension=0, tiled=True),
        lax.psum_scatter(grad_w_key, "fsdp", scatter_dimension=0, tiled=True),
        lax.psum_scatter(grad_w_value, "fsdp", scatter_dimension=0, tiled=True),
        lax.psum_scatter(d_query_norm, "fsdp", scatter_dimension=0, tiled=True),
        lax.psum_scatter(d_key_norm, "fsdp", scatter_dimension=0, tiled=True),
        lax.psum_scatter(grad_w_output, "fsdp", scatter_dimension=0, tiled=True),
        lax.psum_scatter(d_attn_post, "fsdp", scatter_dimension=0, tiled=True),
    )
    column_sums = (
        lax.psum_scatter(attn_sums[1], "ctx", scatter_dimension=1, tiled=True),
        lax.psum_scatter(attn_sums[2], "ctx", scatter_dimension=1, tiled=True),
        lax.psum_scatter(attn_sums[3], "ctx", scatter_dimension=1, tiled=True),
        lax.psum_scatter(attn_sums[6], "ctx", scatter_dimension=1, tiled=True),
        lax.psum_scatter(ffn_sums[1], "ctx", scatter_dimension=1, tiled=True),
        lax.psum_scatter(ffn_sums[2], "ctx", scatter_dimension=1, tiled=True),
        lax.psum_scatter(ffn_sums[3], "ctx", scatter_dimension=1, tiled=True),
    )
    full_columns = (
        lax.all_gather(column_sums[0], "ctx", axis=1, tiled=True),
        lax.all_gather(column_sums[1], "ctx", axis=1, tiled=True),
        lax.all_gather(column_sums[2], "ctx", axis=1, tiled=True),
        lax.all_gather(column_sums[3], "ctx", axis=1, tiled=True),
        lax.all_gather(column_sums[4], "ctx", axis=1, tiled=True),
        lax.all_gather(column_sums[5], "ctx", axis=1, tiled=True),
        lax.all_gather(column_sums[6], "ctx", axis=1, tiled=True),
    )
    gain_totals = lax.psum(
        (attn_sums[0], attn_sums[4], attn_sums[5], attn_sums[7], ffn_sums[0], ffn_sums[4]), "ctx"
    )
    results = (
        gain_totals[0],
        full_columns[0],
        full_columns[1],
        full_columns[2],
        gain_totals[1],
        gain_totals[2],
        full_columns[3],
        gain_totals[3],
        gain_totals[4],
        full_columns[4],
        full_columns[5],
        full_columns[6],
        gain_totals[5],
    )
    out_rows = layer_out.astype(bf16).reshape(1, tok_rows, model_width)
    grad_rows = d_tokens.astype(bf16).reshape(1, tok_rows, model_width)
    return (
        out_rows,
        grad_rows,
        results[0],
        results[1],
        results[2],
        results[3],
        results[4],
        results[5],
        results[6],
        results[7],
        results[8],
        results[9],
        results[10],
        results[11],
        results[12],
    )


VMEM_BYTES = 48 * 1024 * 1024


def peer_of(axis, index):
    return dict(device_id={axis: index}, device_id_type=pl.DeviceIdType.MESH)


class Piece:
    def __init__(self, axis, n, source, result, slots, send, recv):
        self.axis, self.n, self.source, self.result = axis, n, source, result
        self.slots, self.send, self.recv = slots, send, recv
        self.me = lax.axis_index(axis)
        self.outer, self.inner = lax.div(self.me, 2), lax.rem(self.me, 2)
        self.span = n // 2
        self.twin = self.outer * 2 + (1 - self.inner)

    def ahead(self, step):
        return lax.rem(self.outer + step, self.span)

    def behind(self, step):
        return lax.rem(self.outer + self.span - step, self.span)

    def copy(self, source, target_ref, lane, target):
        return pltpu.make_async_remote_copy(
            src_ref=source,
            dst_ref=target_ref,
            send_sem=self.send.at[lane],
            recv_sem=self.recv.at[lane],
            **peer_of(self.axis, target),
        )


class Gather(Piece):
    def out(self, source, slot, lane, target):
        return self.copy(source, self.result.at[slot], lane, target)

    def begin(self):
        for step in range(1, self.span):
            self.out(self.source, self.me, step, self.ahead(step) * 2 + self.inner).start()
        self.out(self.source, self.me, 0, self.twin).start()

    def own(self):
        self.result[self.me] = self.source[...]

    def middle(self):
        for step in range(1, self.span):
            slot = self.behind(step) * 2 + self.inner
            self.out(self.source, slot, step, self.twin).wait_recv()
            self.out(self.result.at[slot], slot, self.span - 1 + step, self.twin).start()

    def end(self):
        self.out(self.source, self.twin, 0, self.twin).wait_recv()
        for step in range(1, self.span):
            slot = self.behind(step) * 2 + (1 - self.inner)
            self.out(self.source, slot, self.span - 1 + step, self.twin).wait_recv()
        for lane in range(2 * self.span - 1):
            self.out(self.source, self.me, lane, self.twin).wait_send()


class Swap(Piece):
    def trade(self, step, slot):
        target = lax.rem(self.me + step, self.n)
        return self.copy(self.source.at[target], self.result.at[slot], step, target)

    def begin(self):
        for step in range(1, self.n):
            self.trade(step, self.me).start()

    def own(self):
        self.result[self.me] = self.source[self.me]

    def middle(self):
        pass

    def end(self):
        for step in range(1, self.n):
            self.trade(step, lax.rem(self.me + self.n - step, self.n)).wait_recv()
        for step in range(1, self.n):
            self.trade(step, self.me).wait_send()


class Sum(Piece):
    def to_twin(self, step):
        block = self.source.at[self.ahead(step) * 2 + (1 - self.inner)]
        return self.copy(block, self.slots[0].at[step], step, self.twin)

    def to_owner(self, step):
        return self.copy(
            self.slots[1].at[step],
            self.slots[2].at[step],
            self.span + step,
            self.ahead(step) * 2 + self.inner,
        )

    def begin(self):
        for step in list(range(1, self.span)) + [0]:
            self.to_twin(step).start()

    def own(self):
        pass

    def middle(self):
        from_twin, paired = self.slots[:2]
        for step in range(1, self.span):
            self.to_twin(step).wait_recv()
            mine = self.source[self.ahead(step) * 2 + self.inner].astype(jnp.float32)
            paired[step] = (mine + from_twin[step].astype(jnp.float32)).astype(paired.dtype)
            self.to_owner(step).start()

    def end(self):
        self.to_twin(0).wait_recv()
        total = self.source[self.me].astype(jnp.float32) + self.slots[0][0].astype(jnp.float32)
        for step in range(1, self.span):
            self.to_owner(step).wait_recv()
            total = total + self.slots[2][step].astype(jnp.float32)
        self.result[...] = total.astype(self.result.dtype)
        for step in range(self.span):
            self.to_twin(step).wait_send()
        for step in range(1, self.span):
            self.to_owner(step).wait_send()


def exchange_kernel(plan, *refs):
    count = len(plan)
    send, recv = refs[-2:]
    slots = list(refs[2 * count : -2])
    pieces = []
    for i, (kind, axis, n) in enumerate(plan):
        own_slots = [slots.pop(0) for _ in range(3)] if kind is Sum else []
        pieces.append(kind(axis, n, refs[i], refs[count + i], own_slots, send.at[i], recv.at[i]))
    barrier = pltpu.get_barrier_semaphore()
    heard = 0
    for axis, n in sorted({(axis, n) for _, axis, n in plan}):
        first = [piece for piece in pieces if piece.axis == axis][0]
        if any(kind is Swap and name == axis for kind, name, _ in plan):
            peers = [lax.rem(first.me + step, n) for step in range(1, n)]
        else:
            peers = [first.twin]
            peers += [first.ahead(step) * 2 + first.inner for step in range(1, n // 2)]
        for peer in peers:
            pl.semaphore_signal(barrier, inc=1, **peer_of(axis, peer))
        heard += len(peers)
    pl.semaphore_wait(barrier, heard)
    for piece in pieces:
        piece.begin()
    for piece in pieces:
        piece.own()
    for piece in pieces:
        piece.middle()
    for piece in pieces:
        piece.end()


def exchange(key, *pieces):
    plan = [(kind, axis, lax.axis_size(axis)) for kind, axis, _, _ in pieces]
    arrays = [piece[2] for piece in pieces]
    spec = pl.BlockSpec(memory_space=pltpu.VMEM)
    shapes, slots = [], []
    for (kind, _, n), (_, _, array, kept) in zip(plan, pieces):
        if kind is Gather:
            shapes.append(jax.ShapeDtypeStruct((n,) + array.shape, kept))
        elif kind is Swap:
            shapes.append(jax.ShapeDtypeStruct(array.shape, kept))
        else:
            shapes.append(jax.ShapeDtypeStruct(array.shape[1:], kept))
            slots += [pltpu.VMEM((n // 2,) + array.shape[1:], array.dtype)] * 3
    lanes = max(n for _, _, n in plan)
    return pl.pallas_call(
        functools.partial(exchange_kernel, plan),
        out_shape=shapes,
        in_specs=[spec] * len(arrays),
        out_specs=[spec] * len(arrays),
        scratch_shapes=slots + [pltpu.SemaphoreType.DMA((len(plan), lanes))] * 2,
        compiler_params=pltpu.CompilerParams(
            collective_id=key, has_side_effects=True, vmem_limit_bytes=VMEM_BYTES
        ),
    )(*arrays)


def finish_kernel(owners, ways, sums, count, *refs):
    ins, outs = refs[:count], refs[count : 2 * count]
    refs = refs[2 * count :]
    from_twin, paired, landed = refs[:sums], refs[sums : 2 * sums], refs[2 * sums : 3 * sums]
    send, recv, send_ctx, recv_ctx = refs[3 * sums :]
    f32 = jnp.float32
    me = lax.axis_index("fsdp")
    outer, inner = lax.div(me, 2), lax.rem(me, 2)
    span = owners // 2
    twin = outer * 2 + (1 - inner)
    part = lax.axis_index("ctx")
    side, core = lax.div(part, 2), lax.rem(part, 2)
    reach = ways // 2
    mate = side * 2 + (1 - core)

    def ahead(step):
        return lax.rem(outer + step, span)

    def across(step):
        return lax.rem(side + step, reach) * 2 + core

    def behind(step):
        return lax.rem(side + reach - step, reach)

    barrier = pltpu.get_barrier_semaphore()
    fsdp_peers = [twin] + [ahead(step) * 2 + inner for step in range(1, span)]
    ctx_peers = [mate] + [across(step) for step in range(1, reach)]
    for index in fsdp_peers:
        pl.semaphore_signal(barrier, inc=1, **peer_of("fsdp", index))
    for index in ctx_peers:
        pl.semaphore_signal(barrier, inc=1, **peer_of("ctx", index))
    pl.semaphore_wait(barrier, len(fsdp_peers) + len(ctx_peers))

    def to_twin(i, step):
        return pltpu.make_async_remote_copy(
            src_ref=ins[i].at[ahead(step) * 2 + (1 - inner)],
            dst_ref=from_twin[i].at[step],
            send_sem=send.at[i, step],
            recv_sem=recv.at[i, step],
            **peer_of("fsdp", twin),
        )

    def to_owner(i, step):
        return pltpu.make_async_remote_copy(
            src_ref=paired[i].at[step],
            dst_ref=landed[i].at[step],
            send_sem=send.at[i, span + step],
            recv_sem=recv.at[i, span + step],
            **peer_of("fsdp", ahead(step) * 2 + inner),
        )

    def spread(i, slot, lane, target):
        return pltpu.make_async_remote_copy(
            src_ref=outs[i].at[slot],
            dst_ref=outs[i].at[slot],
            send_sem=send_ctx.at[i, lane],
            recv_sem=recv_ctx.at[i, lane],
            **peer_of("ctx", target),
        )

    def publish(i):
        for step in range(1, reach):
            spread(i, part, step, across(step)).start()
        spread(i, part, 0, mate).start()

    for i in range(sums):
        for step in list(range(1, span)) + [0]:
            to_twin(i, step).start()
    for i in range(sums, count):
        outs[i][part] = ins[i][...]
        publish(i)
    for i in range(sums):
        for step in range(1, span):
            to_twin(i, step).wait_recv()
            paired[i][step] = (
                ins[i][ahead(step) * 2 + inner].astype(f32) + from_twin[i][step].astype(f32)
            ).astype(paired[i].dtype)
            to_owner(i, step).start()
    for i in range(sums):
        to_twin(i, 0).wait_recv()
        total = ins[i][me].astype(f32) + from_twin[i][0].astype(f32)
        for step in range(1, span):
            to_owner(i, step).wait_recv()
            total = total + landed[i][step].astype(f32)
        outs[i][part] = total.astype(outs[i].dtype)
        publish(i)
    turn = list(range(sums, count)) + list(range(sums))
    for i in turn:
        for step in range(1, reach):
            slot = behind(step) * 2 + core
            spread(i, slot, step, mate).wait_recv()
            spread(i, slot, reach - 1 + step, mate).start()
    for i in turn:
        spread(i, mate, 0, mate).wait_recv()
        for step in range(1, reach):
            spread(i, behind(step) * 2 + (1 - core), reach - 1 + step, mate).wait_recv()
        for lane in range(2 * reach - 1):
            spread(i, part, lane, mate).wait_send()
    for i in range(sums):
        for step in range(span):
            to_twin(i, step).wait_send()
        for step in range(1, span):
            to_owner(i, step).wait_send()


def finish(owners, ways, key, summed, others):
    arrays = summed + others
    sums, count = len(summed), len(arrays)
    spec = pl.BlockSpec(memory_space=pltpu.VMEM)
    shapes = [(ways,) + a.shape[1:] for a in summed] + [(ways,) + a.shape for a in others]
    slots = [pltpu.VMEM((owners // 2,) + a.shape[1:], a.dtype) for a in summed]
    return pl.pallas_call(
        functools.partial(finish_kernel, owners, ways, sums, count),
        out_shape=[jax.ShapeDtypeStruct(shape, a.dtype) for shape, a in zip(shapes, arrays)],
        in_specs=[spec] * count,
        out_specs=[spec] * count,
        scratch_shapes=slots * 3
        + [pltpu.SemaphoreType.DMA((sums, owners))] * 2
        + [pltpu.SemaphoreType.DMA((count, ways - 1))] * 2,
        compiler_params=pltpu.CompilerParams(
            collective_id=key, has_side_effects=True, vmem_limit_bytes=VMEM_BYTES
        ),
    )(*arrays)


def turned_norm(values, gain_vec, cosine, sine_table):
    return rotate(rms_gain(values, gain_vec), cosine, sine_table)


def split_body(
    tokens,
    positions,
    cotangent,
    attn_norm,
    w_query,
    w_key,
    w_value,
    query_norm,
    key_norm,
    w_output,
    attn_post_norm,
    ffn_norm,
    w_gate,
    w_up,
    w_down,
    ffn_post_norm,
):
    f32 = jnp.float32
    bf16 = jnp.bfloat16
    ways = lax.axis_size("ctx")
    owners = lax.axis_size("fsdp")
    part = lax.axis_index("ctx")
    rows, width = tokens.shape[1:]
    seq = rows * ways
    shard = w_query.shape[0]
    hidden_row = w_down.shape[0] // ways
    out_row = w_output.shape[0] // ways
    head_share = query_norm.shape[0]
    hidden_cols = owners * hidden_row
    inputs = tokens.reshape(rows, width).astype(f32)
    grad_out = cotangent.reshape(rows, width).astype(f32)

    def mul(left, right, dims):
        return lax.dot_general(left, right, (dims, ((), ())), preferred_element_type=f32)

    def nn(left, right):
        return mul(left, right, ((1,), (0,)))

    def nt(left, right):
        return mul(left, right, ((1,), (1,)))

    def tn(left, right):
        return mul(left, right, ((0,), (0,)))

    def hidden_part(weight):
        cut = weight.reshape(shard, owners, ways, hidden_row)
        return lax.dynamic_index_in_dim(cut, part, 2, keepdims=False).reshape(
            shard, owners * hidden_row
        )

    def hidden_whole(parts):
        return (
            parts.reshape(ways, shard, owners, hidden_row)
            .transpose(1, 2, 0, 3)
            .reshape(shard, owners * ways * hidden_row)
        )

    gain_row = jnp.concatenate(
        [attn_norm, attn_post_norm, ffn_norm, ffn_post_norm, query_norm, key_norm]
    )
    gain_size = gain_row.shape[0]
    attn_pack = jnp.concatenate(
        [
            jnp.concatenate(
                [lax.dynamic_slice_in_dim(w_query, part * HD, HD, 1), w_key, w_value], axis=1
            ),
            jnp.pad(gain_row[None], ((0, 15), (0, 3 * HD - gain_size))),
        ],
        axis=0,
    )
    hidden_cols = owners * hidden_row
    attn_all, wo_rows = exchange(
        0,
        (Gather, "fsdp", attn_pack, bf16),
        (
            Gather,
            "fsdp",
            lax.dynamic_slice_in_dim(w_output, part * out_row, out_row, 0),
            bf16,
        ),
    )
    gains = attn_all[:, shard, :gain_size].astype(f32)

    def gain_of(index):
        return gains[:, index * shard : (index + 1) * shard].reshape(width)

    g_attn, g_post, g_ffn, g_ffn_post = (gain_of(index) for index in range(4))
    g_query = gains[:, 4 * shard : 4 * shard + head_share].reshape(HD)
    g_key = gains[:, 4 * shard + head_share :].reshape(HD)
    w_qkv = attn_all[:, :shard].reshape(width, 3 * HD)
    wq_head, wk_full, wv_full = (w_qkv[:, i * HD : (i + 1) * HD] for i in range(3))
    attn_in = rms_gain(inputs, g_attn).astype(bf16)
    attn_seq, place_all, wo_head, wg_all = exchange(
        2,
        (Gather, "ctx", attn_in, bf16),
        (Gather, "ctx", jnp.broadcast_to(positions.reshape(1, rows), (8, rows)), jnp.int32),
        (Swap, "ctx", wo_rows.reshape(ways, owners // ways * out_row, width), bf16),
        (Gather, "fsdp", hidden_part(w_gate), bf16),
    )
    wg_part = wg_all.reshape(width, hidden_cols)
    wo_head = (
        wo_head.reshape(ways, owners // ways, out_row, width)
        .transpose(1, 0, 2, 3)
        .reshape(HD, width)
    )
    attn_seq = attn_seq.reshape(seq, width)
    seq_place = place_all[:, 0].reshape(seq)
    index = jnp.arange(seq, dtype=jnp.int32)
    key_mask = (
        (index[None, :] <= index[:, None])
        & (index[:, None] - index[None, :] < WINDOW)
        & (index[None, :] >= (index - seq_place)[:, None])
    )
    cosine, sine_table = rope_tables(seq_place)
    cosine, sine_table = cosine[:, 0], sine_table[:, 0]
    qkv = nn(attn_seq, w_qkv)
    q_pre, k_pre, v_pre = (qkv[:, i * HD : (i + 1) * HD] for i in range(3))
    v_low = v_pre.astype(bf16)
    q_low = turned_norm(q_pre, g_query, cosine, sine_table).astype(bf16)
    k_low = turned_norm(k_pre, g_key, cosine, sine_table).astype(bf16)
    scores = jnp.where(key_mask, nt(q_low, k_low) * ATTN_SCALE, NEGATIVE)
    shifted = jnp.exp(scores - jnp.max(scores, axis=-1, keepdims=True))
    prob_rows = shifted / jnp.sum(shifted, axis=-1, keepdims=True)
    prob_low = prob_rows.astype(bf16)
    att_low = nn(prob_low, v_low).astype(bf16)

    def by_rows(value):
        return value.astype(bf16).reshape(ways, rows, value.shape[1])

    def blocks(value):
        return value.astype(bf16).reshape(owners, value.shape[0] // owners, value.shape[1])

    branch, wu_all = exchange(
        3,
        (Sum, "ctx", by_rows(nn(att_low, wo_head)), f32),
        (Gather, "fsdp", hidden_part(w_up), bf16),
    )
    wu_part = wu_all.reshape(width, hidden_cols)
    hidden_res = inputs + rms_gain(branch, g_post)
    ffn_seq, wd_all = exchange(
        4,
        (Gather, "ctx", rms_gain(hidden_res, g_ffn).astype(bf16), bf16),
        (
            Gather,
            "fsdp",
            lax.dynamic_slice_in_dim(w_down, part * hidden_row, hidden_row, 0),
            bf16,
        ),
    )
    ffn_seq = ffn_seq.reshape(seq, width)
    wd_part = wd_all.reshape(hidden_cols, width)
    gate_proj = nn(ffn_seq, wg_part)
    up_proj = nn(ffn_seq, wu_part)
    mixed_low = gated_gelu(gate_proj, up_proj).astype(bf16)
    (down_out,) = exchange(5, (Sum, "ctx", by_rows(nn(mixed_low, wd_part)), f32))
    layer_out = hidden_res + rms_gain(down_out, g_ffn_post)

    d_down, d_ffn_post = jax.vjp(rms_gain, down_out, g_ffn_post)[1](grad_out)
    d_down_seq = exchange(6, (Gather, "ctx", d_down.astype(bf16), bf16))[0].reshape(seq, width)
    d_mixed = nt(d_down_seq, wd_part)
    d_gate, d_up = jax.vjp(gated_gelu, gate_proj, up_proj)[1](d_mixed)
    d_gate_low = d_gate.astype(bf16)
    d_up_low = d_up.astype(bf16)
    d_ffn_in, wd_g = exchange(
        7,
        (Sum, "ctx", by_rows(nt(d_gate_low, wg_part) + nt(d_up_low, wu_part)), f32),
        (Sum, "fsdp", blocks(tn(mixed_low, d_down_seq)), bf16),
    )
    d_hidden_part, d_ffn_norm = jax.vjp(rms_gain, hidden_res, g_ffn)[1](d_ffn_in)
    d_hidden = grad_out + d_hidden_part

    d_branch, d_post = jax.vjp(rms_gain, branch, g_post)[1](d_hidden)
    d_branch_seq, wg_g = exchange(
        8,
        (Gather, "ctx", d_branch.astype(bf16), bf16),
        (Sum, "fsdp", blocks(tn(ffn_seq, d_gate_low)), bf16),
    )
    d_branch_seq = d_branch_seq.reshape(seq, width)
    grad_w_output = tn(att_low, d_branch_seq)
    d_att = nt(d_branch_seq, wo_head).astype(bf16)
    d_values = tn(prob_low, d_att)
    d_probs = nt(d_att, v_low)
    d_scores = prob_rows * (d_probs - jnp.sum(prob_rows * d_probs, axis=-1, keepdims=True))
    d_scores_low = d_scores.astype(bf16)
    d_queries = nn(d_scores_low, k_low) * ATTN_SCALE
    d_keys = tn(d_scores_low, q_low) * ATTN_SCALE
    d_q_pre, d_query_norm = jax.vjp(
        lambda values, gain_vec: turned_norm(values, gain_vec, cosine, sine_table), q_pre, g_query
    )[1](d_queries)
    dq_low = d_q_pre.astype(bf16)
    sums, wu_g = exchange(
        9,
        (
            Sum,
            "ctx",
            by_rows(jnp.concatenate([nt(dq_low, wq_head), d_keys, d_values], axis=1)),
            f32,
        ),
        (Sum, "fsdp", blocks(tn(ffn_seq, d_up_low)), bf16),
    )
    own_cos = lax.dynamic_slice_in_dim(cosine, part * rows, rows, 0)
    own_sin = lax.dynamic_slice_in_dim(sine_table, part * rows, rows, 0)
    own_k = lax.dynamic_slice_in_dim(k_pre, part * rows, rows, 0)
    d_k_pre, d_key_norm = jax.vjp(
        lambda values, gain_vec: turned_norm(values, gain_vec, own_cos, own_sin), own_k, g_key
    )[1](sums[:, width : width + HD])
    dkv_low = jnp.concatenate([d_k_pre, sums[:, width + HD :]], axis=1).astype(bf16)
    d_attn_in = sums[:, :width] + nt(dkv_low, w_qkv[:, HD:])
    dkv_seq, grad_wo_rows, wq_g = exchange(
        10,
        (Gather, "ctx", dkv_low, bf16),
        (
            Swap,
            "ctx",
            grad_w_output.astype(bf16)
            .reshape(owners // ways, ways, out_row, width)
            .transpose(1, 0, 2, 3)
            .reshape(ways, owners // ways * out_row, width),
            bf16,
        ),
        (Sum, "fsdp", blocks(tn(attn_seq, dq_low)), bf16),
    )
    dkv_seq = dkv_seq.reshape(seq, 2 * HD)
    grad_wo_rows = grad_wo_rows.reshape(owners, out_row, width)
    d_inputs_part, d_attn_norm = jax.vjp(rms_gain, inputs, g_attn)[1](d_attn_in)
    d_tokens = d_hidden + d_inputs_part
    dkv_cols = 2 * HD // ways
    grad_w_kv = tn(attn_seq, lax.dynamic_slice_in_dim(dkv_seq, part * dkv_cols, dkv_cols, 1))

    gain_grads = jnp.concatenate(
        [
            value.reshape(owners, -1)
            for value in (d_attn_norm, d_post, d_ffn_norm, d_ffn_post, d_query_norm, d_key_norm)
        ],
        axis=1,
    )
    gain_grads = jnp.pad(gain_grads[:, None], ((0, 0), (0, 15), (0, 0)))

    wo_g, wkv_g, gain_g, wg_g, wu_g, wd_g, wq_g = finish(
        owners,
        ways,
        12,
        [grad_wo_rows, blocks(grad_w_kv), gain_grads.astype(bf16)],
        [wg_g, wu_g, wd_g, wq_g],
    )
    gain_sum = jnp.sum(gain_g[:, 0].astype(f32), axis=0)
    ends = [shard * i for i in range(1, 5)] + [4 * shard + head_share]
    t_attn, t_post, t_ffn, t_ffn_post, t_query, t_key = jnp.split(gain_sum, ends)
    half = ways // 2

    def columns(parts):
        return parts.transpose(1, 0, 2).reshape(shard, -1).astype(f32)

    return (
        layer_out.astype(bf16).reshape(1, rows, width),
        d_tokens.astype(bf16).reshape(1, rows, width),
        t_attn,
        columns(wq_g),
        columns(wkv_g[:half]),
        columns(wkv_g[half:]),
        t_query,
        t_key,
        wo_g.reshape(ways * out_row, width).astype(f32),
        t_post,
        t_ffn,
        hidden_whole(wg_g).astype(f32),
        hidden_whole(wu_g).astype(f32),
        wd_g.reshape(ways * hidden_row, width).astype(f32),
        t_ffn_post,
    )


def solution(mesh):
    return jax.shard_map(
        plain_body if mesh.shape['ctx'] != HQ or mesh.shape['fsdp'] != 2 * HQ else split_body,
        mesh=mesh,
        in_specs=(
            P("fsdp", "ctx", None),
            P("fsdp", "ctx"),
            P("fsdp", "ctx", None),
            P("fsdp"),
            P("fsdp", None),
            P("fsdp", None),
            P("fsdp", None),
            P("fsdp"),
            P("fsdp"),
            P("fsdp", None),
            P("fsdp"),
            P("fsdp"),
            P("fsdp", None),
            P("fsdp", None),
            P("fsdp", None),
            P("fsdp"),
        ),
        out_specs=(
            P("fsdp", "ctx", None),
            P("fsdp", "ctx", None),
            P("fsdp"),
            P("fsdp", None),
            P("fsdp", None),
            P("fsdp", None),
            P("fsdp"),
            P("fsdp"),
            P("fsdp", None),
            P("fsdp"),
            P("fsdp"),
            P("fsdp", None),
            P("fsdp", None),
            P("fsdp", None),
            P("fsdp"),
        ),
        check_vma=False,
    )
```

```python
import functools

import jax
import jax.numpy as jnp
from jax import lax
from jax.experimental import pallas as pl
from jax.experimental.pallas import tpu as pltpu
from jax.sharding import PartitionSpec as P

HQ = 4
HD = 256
WINDOW = 512


EPSILON = 1e-06
ATTN_SCALE = 0.0625
NEGATIVE = -1e30


def shifted_2(value, axis, steps):
    count = lax.axis_size(axis)
    leading, last = (max(0, -steps), min(count, count - steps))
    return lax.ppermute(value, axis, [(source, source + steps) for source in range(leading, last)])


def rms_gain(values, gain_vec):
    return (
        values * lax.rsqrt(jnp.mean(values * values, axis=-1, keepdims=True) + EPSILON) * gain_vec
    )


def rope_tables(seq_place):
    half_width = HD // 2
    inverse = jnp.power(10000.0, -jnp.arange(half_width, dtype=jnp.float32) * (2.0 / HD))
    angles = seq_place.astype(jnp.float32)[:, None] * inverse[None, :]
    return (jnp.cos(angles)[:, None, :], jnp.sin(angles)[:, None, :])


def rotate(values, cosine, sine_table):
    half_width = values.shape[-1] // 2
    front_half = values[..., :half_width]
    back_half = values[..., half_width:]
    return jnp.concatenate(
        [
            front_half * cosine - back_half * sine_table,
            back_half * cosine + front_half * sine_table,
        ],
        axis=-1,
    )


def query_key(q_pre, k_pre, g_query, g_key, cosine, sine_table):
    return (
        rotate(rms_gain(q_pre, g_query), cosine, sine_table),
        rotate(rms_gain(k_pre, g_key), cosine, sine_table),
    )


def gated_gelu(gate_proj, up_proj):
    return jax.nn.gelu(gate_proj, approximate=True) * up_proj


def masked_scores(q_low, key_rows, key_mask):
    raw_scores = (
        jnp.einsum("thd,kd->htk", q_low, key_rows, preferred_element_type=jnp.float32) * ATTN_SCALE
    )
    return jnp.where(key_mask[None], raw_scores, NEGATIVE)


def plain_body(
    tokens,
    positions,
    cotangent,
    attn_norm,
    w_query,
    w_key,
    w_value,
    query_norm,
    key_norm,
    w_output,
    attn_post_norm,
    ffn_norm,
    w_gate,
    w_up,
    w_down,
    ffn_post_norm,
):
    f32 = jnp.float32
    bf16 = jnp.bfloat16
    tok_rows = tokens.shape[1]
    model_width = tokens.shape[2]
    inputs = tokens.reshape(tok_rows, model_width).astype(f32)
    grad_out = cotangent.reshape(tok_rows, model_width).astype(f32)
    seq_place = positions.reshape(tok_rows)
    g_attn, wq_full, wk_full, wv_full, gq_full, gk_full, wo_full, g_attn_post = (
        lax.all_gather(attn_norm, "fsdp", axis=0, tiled=True),
        lax.all_gather(w_query, "fsdp", axis=0, tiled=True),
        lax.all_gather(w_key, "fsdp", axis=0, tiled=True),
        lax.all_gather(w_value, "fsdp", axis=0, tiled=True),
        lax.all_gather(query_norm, "fsdp", axis=0, tiled=True),
        lax.all_gather(key_norm, "fsdp", axis=0, tiled=True),
        lax.all_gather(w_output, "fsdp", axis=0, tiled=True),
        lax.all_gather(attn_post_norm, "fsdp", axis=0, tiled=True),
    )
    block_index = lax.axis_index("ctx")
    halo_count = -(-WINDOW // tok_rows)
    query_index = block_index * tok_rows + jnp.arange(tok_rows, dtype=jnp.int32)
    key_index = block_index * tok_rows + jnp.arange(
        -halo_count * tok_rows, tok_rows, dtype=jnp.int32
    )
    key_mask = (
        (key_index[None, :] <= query_index[:, None])
        & (query_index[:, None] - key_index[None, :] < WINDOW)
        & (key_index[None, :] >= (query_index - seq_place)[:, None])
    )
    attn_in = rms_gain(inputs, g_attn.astype(f32)).astype(bf16)
    q_pre = jnp.dot(attn_in, wq_full, preferred_element_type=f32).reshape(tok_rows, HQ, HD)
    k_pre = jnp.dot(attn_in, wk_full, preferred_element_type=f32).reshape(tok_rows, 1, HD)
    v_low = jnp.dot(attn_in, wv_full, preferred_element_type=f32).astype(bf16)
    cosine, sine_table = rope_tables(seq_place)
    gq_gain = gq_full.astype(f32)
    gk_gain = gk_full.astype(f32)
    q_turned, k_turned = query_key(q_pre, k_pre, gq_gain, gk_gain, cosine, sine_table)
    q_low = q_turned.astype(bf16)
    k_low = k_turned.reshape(tok_rows, HD).astype(bf16)
    key_parts = []
    value_parts = []
    for distance in range(halo_count, 0, -1):
        got_keys, got_values = shifted_2((k_low, v_low), "ctx", distance)
        key_parts.append(got_keys)
        value_parts.append(got_values)
    key_rows = jnp.concatenate(key_parts + [k_low], axis=0)
    value_rows = jnp.concatenate(value_parts + [v_low], axis=0)
    scores = masked_scores(q_low, key_rows, key_mask)
    row_max = jnp.max(scores, axis=-1, keepdims=True)
    shifted = jnp.exp(scores - row_max)
    row_total = jnp.sum(shifted, axis=-1, keepdims=True)
    log_total = row_max + jnp.log(row_total)
    prob_low = (shifted / row_total).astype(bf16)
    attended = jnp.einsum("htk,kd->thd", prob_low, value_rows, preferred_element_type=f32)
    att_low = attended.reshape(tok_rows, HQ * HD).astype(bf16)
    attn_branch = jnp.dot(att_low, wo_full, preferred_element_type=f32)
    g_post_gain = g_attn_post.astype(f32)
    hidden_res = inputs + rms_gain(attn_branch, g_post_gain)
    g_ffn, wg_full, wu_full, wd_full, g_ffn_post = (
        lax.all_gather(ffn_norm, "fsdp", axis=0, tiled=True),
        lax.all_gather(w_gate, "fsdp", axis=0, tiled=True),
        lax.all_gather(w_up, "fsdp", axis=0, tiled=True),
        lax.all_gather(w_down, "fsdp", axis=0, tiled=True),
        lax.all_gather(ffn_post_norm, "fsdp", axis=0, tiled=True),
    )
    g_ffn_gain = g_ffn.astype(f32)
    g_ffn_post_gain = g_ffn_post.astype(f32)
    ffn_in = rms_gain(hidden_res, g_ffn_gain).astype(bf16)
    gate_proj = jnp.dot(ffn_in, wg_full, preferred_element_type=f32)
    up_proj = jnp.dot(ffn_in, wu_full, preferred_element_type=f32)
    mixed_low = gated_gelu(gate_proj, up_proj).astype(bf16)
    down_out = jnp.dot(mixed_low, wd_full, preferred_element_type=f32)
    layer_out = hidden_res + rms_gain(down_out, g_ffn_post_gain)
    g_ffn, wg_full, wu_full, wd_full, g_ffn_post = (
        lax.all_gather(ffn_norm, "fsdp", axis=0, tiled=True),
        lax.all_gather(w_gate, "fsdp", axis=0, tiled=True),
        lax.all_gather(w_up, "fsdp", axis=0, tiled=True),
        lax.all_gather(w_down, "fsdp", axis=0, tiled=True),
        lax.all_gather(ffn_post_norm, "fsdp", axis=0, tiled=True),
    )
    unused, post_ffn_back = jax.vjp(rms_gain, down_out, g_ffn_post_gain)
    d_down, d_ffn_post = post_ffn_back(grad_out)
    d_down_low = d_down.astype(bf16)
    grad_w_down = jnp.einsum("tf,td->fd", mixed_low, d_down_low, preferred_element_type=f32)
    d_mixed = jnp.einsum("td,fd->tf", d_down_low, wd_full, preferred_element_type=f32)
    unused, glu_back = jax.vjp(gated_gelu, gate_proj, up_proj)
    d_gate, d_up = glu_back(d_mixed)
    d_gate_low = d_gate.astype(bf16)
    d_up_low = d_up.astype(bf16)
    grad_w_gate = jnp.einsum("td,tf->df", ffn_in, d_gate_low, preferred_element_type=f32)
    grad_w_up = jnp.einsum("td,tf->df", ffn_in, d_up_low, preferred_element_type=f32)
    d_ffn_in = jnp.einsum(
        "tf,df->td", d_gate_low, wg_full, preferred_element_type=f32
    ) + jnp.einsum("tf,df->td", d_up_low, wu_full, preferred_element_type=f32)
    unused, ffn_norm_back = jax.vjp(rms_gain, hidden_res, g_ffn_gain)
    d_hidden_part, d_ffn_norm = ffn_norm_back(d_ffn_in)
    d_hidden = grad_out + d_hidden_part
    ffn_sums = (
        lax.psum_scatter(d_ffn_norm, "fsdp", scatter_dimension=0, tiled=True),
        lax.psum_scatter(grad_w_gate, "fsdp", scatter_dimension=0, tiled=True),
        lax.psum_scatter(grad_w_up, "fsdp", scatter_dimension=0, tiled=True),
        lax.psum_scatter(grad_w_down, "fsdp", scatter_dimension=0, tiled=True),
        lax.psum_scatter(d_ffn_post, "fsdp", scatter_dimension=0, tiled=True),
    )
    g_attn, wq_full, wk_full, wv_full, gq_full, gk_full, wo_full, g_attn_post = (
        lax.all_gather(attn_norm, "fsdp", axis=0, tiled=True),
        lax.all_gather(w_query, "fsdp", axis=0, tiled=True),
        lax.all_gather(w_key, "fsdp", axis=0, tiled=True),
        lax.all_gather(w_value, "fsdp", axis=0, tiled=True),
        lax.all_gather(query_norm, "fsdp", axis=0, tiled=True),
        lax.all_gather(key_norm, "fsdp", axis=0, tiled=True),
        lax.all_gather(w_output, "fsdp", axis=0, tiled=True),
        lax.all_gather(attn_post_norm, "fsdp", axis=0, tiled=True),
    )
    unused, post_attn_back = jax.vjp(rms_gain, attn_branch, g_post_gain)
    d_branch, d_attn_post = post_attn_back(d_hidden)
    d_branch_low = d_branch.astype(bf16)
    grad_w_output = jnp.einsum("tc,td->cd", att_low, d_branch_low, preferred_element_type=f32)
    d_attended = (
        jnp.einsum("td,cd->tc", d_branch_low, wo_full, preferred_element_type=f32)
        .reshape(tok_rows, HQ, HD)
        .astype(bf16)
    )
    scores = masked_scores(q_low, key_rows, key_mask)
    prob_rows = jnp.exp(scores - log_total)
    prob_low = prob_rows.astype(bf16)
    d_values = jnp.einsum("htk,thd->kd", prob_low, d_attended, preferred_element_type=f32)
    d_probs = jnp.einsum("thd,kd->htk", d_attended, value_rows, preferred_element_type=f32)
    d_scores = prob_rows * (d_probs - jnp.sum(prob_rows * d_probs, axis=-1, keepdims=True))
    d_scores_low = d_scores.astype(bf16)
    d_queries = (
        jnp.einsum("htk,kd->thd", d_scores_low, key_rows, preferred_element_type=f32) * ATTN_SCALE
    )
    d_keys = jnp.einsum("htk,thd->kd", d_scores_low, q_low, preferred_element_type=f32) * ATTN_SCALE
    own_keys = d_keys[halo_count * tok_rows :]
    own_values = d_values[halo_count * tok_rows :]
    for distance in range(halo_count, 0, -1):
        part_index = halo_count - distance
        back_keys, back_values = shifted_2(
            (
                d_keys[part_index * tok_rows : (part_index + 1) * tok_rows],
                d_values[part_index * tok_rows : (part_index + 1) * tok_rows],
            ),
            "ctx",
            -distance,
        )
        own_keys = own_keys + back_keys
        own_values = own_values + back_values
    unused, turn_back = jax.vjp(
        lambda q_in, k_in, gq_in, gk_in: query_key(q_in, k_in, gq_in, gk_in, cosine, sine_table),
        q_pre,
        k_pre,
        gq_gain,
        gk_gain,
    )
    d_q_pre, d_k_pre, d_query_norm, d_key_norm = turn_back(
        (d_queries, own_keys.reshape(tok_rows, 1, HD))
    )
    dq_low = d_q_pre.reshape(tok_rows, HQ * HD).astype(bf16)
    dk_low = d_k_pre.reshape(tok_rows, HD).astype(bf16)
    dv_low = own_values.astype(bf16)
    grad_w_query = jnp.einsum("td,tc->dc", attn_in, dq_low, preferred_element_type=f32)
    grad_w_key = jnp.einsum("td,tc->dc", attn_in, dk_low, preferred_element_type=f32)
    grad_w_value = jnp.einsum("td,tc->dc", attn_in, dv_low, preferred_element_type=f32)
    d_attn_in = (
        jnp.einsum("tc,dc->td", dq_low, wq_full, preferred_element_type=f32)
        + jnp.einsum("tc,dc->td", dk_low, wk_full, preferred_element_type=f32)
        + jnp.einsum("tc,dc->td", dv_low, wv_full, preferred_element_type=f32)
    )
    unused, first_back = jax.vjp(rms_gain, inputs, g_attn.astype(f32))
    d_inputs_part, d_attn_norm = first_back(d_attn_in)
    d_tokens = d_hidden + d_inputs_part
    attn_sums = (
        lax.psum_scatter(d_attn_norm, "fsdp", scatter_dimension=0, tiled=True),
        lax.psum_scatter(grad_w_query, "fsdp", scatter_dimension=0, tiled=True),
        lax.psum_scatter(grad_w_key, "fsdp", scatter_dimension=0, tiled=True),
        lax.psum_scatter(grad_w_value, "fsdp", scatter_dimension=0, tiled=True),
        lax.psum_scatter(d_query_norm, "fsdp", scatter_dimension=0, tiled=True),
        lax.psum_scatter(d_key_norm, "fsdp", scatter_dimension=0, tiled=True),
        lax.psum_scatter(grad_w_output, "fsdp", scatter_dimension=0, tiled=True),
        lax.psum_scatter(d_attn_post, "fsdp", scatter_dimension=0, tiled=True),
    )
    column_sums = (
        lax.psum_scatter(attn_sums[1], "ctx", scatter_dimension=1, tiled=True),
        lax.psum_scatter(attn_sums[2], "ctx", scatter_dimension=1, tiled=True),
        lax.psum_scatter(attn_sums[3], "ctx", scatter_dimension=1, tiled=True),
        lax.psum_scatter(attn_sums[6], "ctx", scatter_dimension=1, tiled=True),
        lax.psum_scatter(ffn_sums[1], "ctx", scatter_dimension=1, tiled=True),
        lax.psum_scatter(ffn_sums[2], "ctx", scatter_dimension=1, tiled=True),
        lax.psum_scatter(ffn_sums[3], "ctx", scatter_dimension=1, tiled=True),
    )
    full_columns = (
        lax.all_gather(column_sums[0], "ctx", axis=1, tiled=True),
        lax.all_gather(column_sums[1], "ctx", axis=1, tiled=True),
        lax.all_gather(column_sums[2], "ctx", axis=1, tiled=True),
        lax.all_gather(column_sums[3], "ctx", axis=1, tiled=True),
        lax.all_gather(column_sums[4], "ctx", axis=1, tiled=True),
        lax.all_gather(column_sums[5], "ctx", axis=1, tiled=True),
        lax.all_gather(column_sums[6], "ctx", axis=1, tiled=True),
    )
    gain_totals = lax.psum(
        (attn_sums[0], attn_sums[4], attn_sums[5], attn_sums[7], ffn_sums[0], ffn_sums[4]), "ctx"
    )
    results = (
        gain_totals[0],
        full_columns[0],
        full_columns[1],
        full_columns[2],
        gain_totals[1],
        gain_totals[2],
        full_columns[3],
        gain_totals[3],
        gain_totals[4],
        full_columns[4],
        full_columns[5],
        full_columns[6],
        gain_totals[5],
    )
    out_rows = layer_out.astype(bf16).reshape(1, tok_rows, model_width)
    grad_rows = d_tokens.astype(bf16).reshape(1, tok_rows, model_width)
    return (
        out_rows,
        grad_rows,
        results[0],
        results[1],
        results[2],
        results[3],
        results[4],
        results[5],
        results[6],
        results[7],
        results[8],
        results[9],
        results[10],
        results[11],
        results[12],
    )


VMEM_BYTES = 48 * 1024 * 1024


def peer_of(axis, index):
    return dict(device_id={axis: index}, device_id_type=pl.DeviceIdType.MESH)


class Piece:
    def __init__(self, axis, n, source, result, slots, send, recv):
        self.axis, self.n, self.source, self.result = axis, n, source, result
        self.slots, self.send, self.recv = slots, send, recv
        self.me = lax.axis_index(axis)
        self.outer, self.inner = lax.div(self.me, 2), lax.rem(self.me, 2)
        self.span = n // 2
        self.twin = self.outer * 2 + (1 - self.inner)

    def ahead(self, step):
        return lax.rem(self.outer + step, self.span)

    def behind(self, step):
        return lax.rem(self.outer + self.span - step, self.span)

    def copy(self, source, target_ref, lane, target):
        return pltpu.make_async_remote_copy(
            src_ref=source,
            dst_ref=target_ref,
            send_sem=self.send.at[lane],
            recv_sem=self.recv.at[lane],
            **peer_of(self.axis, target),
        )


def row_cuts(axis, rows):
    cuts = min(3, rows // 16) if axis == "fsdp" else 1
    edges = [rows // 16 * cut // cuts * 16 for cut in range(cuts)] + [rows]
    return [(low, high - low) for low, high in zip(edges, edges[1:])]


class Gather(Piece):
    def rounds(self):
        return len(row_cuts(self.axis, self.source.shape[0]))

    def out(self, cut, handed, slot, lane, target):
        low, size = row_cuts(self.axis, self.source.shape[0])[cut]
        here = pl.ds(low, size)
        there = self.result.at[slot, here]
        source = there if handed else self.source.at[here]
        return self.copy(source, there, cut * (2 * self.span - 1) + lane, target)

    def begin(self):
        for cut in range(self.rounds()):
            for step in range(1, self.span):
                target = self.ahead(step) * 2 + self.inner
                self.out(cut, False, self.me, step, target).start()
            self.out(cut, False, self.me, 0, self.twin).start()

    def own(self):
        self.result[self.me] = self.source[...]

    def middle(self, cut):
        for step in range(1, self.span):
            slot = self.behind(step) * 2 + self.inner
            self.out(cut, False, slot, step, self.twin).wait_recv()
            self.out(cut, True, slot, self.span - 1 + step, self.twin).start()

    def end(self):
        for cut in range(self.rounds()):
            self.out(cut, False, self.twin, 0, self.twin).wait_recv()
            for step in range(1, self.span):
                slot = self.behind(step) * 2 + (1 - self.inner)
                self.out(cut, False, slot, self.span - 1 + step, self.twin).wait_recv()
            for lane in range(2 * self.span - 1):
                self.out(cut, False, self.me, lane, self.twin).wait_send()


class Swap(Piece):
    def trade(self, step, slot):
        target = lax.rem(self.me + step, self.n)
        return self.copy(self.source.at[target], self.result.at[slot], step, target)

    def begin(self):
        for step in range(1, self.n):
            self.trade(step, self.me).start()

    def own(self):
        self.result[self.me] = self.source[self.me]

    def rounds(self):
        return 1

    def middle(self, cut):
        pass

    def end(self):
        for step in range(1, self.n):
            self.trade(step, lax.rem(self.me + self.n - step, self.n)).wait_recv()
        for step in range(1, self.n):
            self.trade(step, self.me).wait_send()


class Sum(Piece):
    def to_twin(self, step):
        block = self.source.at[self.ahead(step) * 2 + (1 - self.inner)]
        return self.copy(block, self.slots[0].at[step], step, self.twin)

    def to_owner(self, step):
        return self.copy(
            self.slots[1].at[step],
            self.slots[2].at[step],
            self.span + step,
            self.ahead(step) * 2 + self.inner,
        )

    def begin(self):
        for step in list(range(1, self.span)) + [0]:
            self.to_twin(step).start()

    def own(self):
        pass

    def rounds(self):
        return 1

    def middle(self, cut):
        from_twin, paired = self.slots[:2]
        for step in range(1, self.span):
            self.to_twin(step).wait_recv()
            mine = self.source[self.ahead(step) * 2 + self.inner].astype(jnp.float32)
            paired[step] = (mine + from_twin[step].astype(jnp.float32)).astype(paired.dtype)
            self.to_owner(step).start()

    def end(self):
        self.to_twin(0).wait_recv()
        total = self.source[self.me].astype(jnp.float32) + self.slots[0][0].astype(jnp.float32)
        for step in range(1, self.span):
            self.to_owner(step).wait_recv()
            total = total + self.slots[2][step].astype(jnp.float32)
        self.result[...] = total.astype(self.result.dtype)
        for step in range(self.span):
            self.to_twin(step).wait_send()
        for step in range(1, self.span):
            self.to_owner(step).wait_send()


def exchange_kernel(plan, *refs):
    count = len(plan)
    send, recv = refs[-2:]
    slots = list(refs[2 * count : -2])
    pieces = []
    for i, (kind, axis, n) in enumerate(plan):
        own_slots = [slots.pop(0) for _ in range(3)] if kind is Sum else []
        pieces.append(kind(axis, n, refs[i], refs[count + i], own_slots, send.at[i], recv.at[i]))
    barrier = pltpu.get_barrier_semaphore()
    heard = 0
    for axis, n in sorted({(axis, n) for _, axis, n in plan}):
        first = [piece for piece in pieces if piece.axis == axis][0]
        if any(kind is Swap and name == axis for kind, name, _ in plan):
            peers = [lax.rem(first.me + step, n) for step in range(1, n)]
        else:
            peers = [first.twin]
            peers += [first.ahead(step) * 2 + first.inner for step in range(1, n // 2)]
        for peer in peers:
            pl.semaphore_signal(barrier, inc=1, **peer_of(axis, peer))
        heard += len(peers)
    pl.semaphore_wait(barrier, heard)
    for piece in pieces:
        piece.begin()
    for piece in pieces:
        piece.own()
    for cut in range(max(piece.rounds() for piece in pieces)):
        for piece in pieces:
            if cut < piece.rounds():
                piece.middle(cut)
    for piece in pieces:
        piece.end()


def exchange(key, *pieces):
    plan = [(kind, axis, lax.axis_size(axis)) for kind, axis, _, _ in pieces]
    arrays = [piece[2] for piece in pieces]
    spec = pl.BlockSpec(memory_space=pltpu.VMEM)
    shapes, slots = [], []
    for (kind, _, n), (_, _, array, kept) in zip(plan, pieces):
        if kind is Gather:
            shapes.append(jax.ShapeDtypeStruct((n,) + array.shape, kept))
        elif kind is Swap:
            shapes.append(jax.ShapeDtypeStruct(array.shape, kept))
        else:
            shapes.append(jax.ShapeDtypeStruct(array.shape[1:], kept))
            slots += [pltpu.VMEM((n // 2,) + array.shape[1:], array.dtype)] * 3
    lanes = 3 * max(n for _, _, n in plan)
    return pl.pallas_call(
        functools.partial(exchange_kernel, plan),
        out_shape=shapes,
        in_specs=[spec] * len(arrays),
        out_specs=[spec] * len(arrays),
        scratch_shapes=slots + [pltpu.SemaphoreType.DMA((len(plan), lanes))] * 2,
        compiler_params=pltpu.CompilerParams(
            collective_id=key, has_side_effects=True, vmem_limit_bytes=VMEM_BYTES
        ),
    )(*arrays)


def finish_kernel(owners, ways, sums, count, *refs):
    ins, outs = refs[:count], refs[count : 2 * count]
    refs = refs[2 * count :]
    from_twin, paired, landed = refs[:sums], refs[sums : 2 * sums], refs[2 * sums : 3 * sums]
    send, recv, send_ctx, recv_ctx = refs[3 * sums :]
    f32 = jnp.float32
    me = lax.axis_index("fsdp")
    outer, inner = lax.div(me, 2), lax.rem(me, 2)
    span = owners // 2
    twin = outer * 2 + (1 - inner)
    part = lax.axis_index("ctx")
    side, core = lax.div(part, 2), lax.rem(part, 2)
    reach = ways // 2
    mate = side * 2 + (1 - core)

    def ahead(step):
        return lax.rem(outer + step, span)

    def across(step):
        return lax.rem(side + step, reach) * 2 + core

    def behind(step):
        return lax.rem(side + reach - step, reach)

    barrier = pltpu.get_barrier_semaphore()
    fsdp_peers = [twin] + [ahead(step) * 2 + inner for step in range(1, span)]
    ctx_peers = [mate] + [across(step) for step in range(1, reach)]
    for index in fsdp_peers:
        pl.semaphore_signal(barrier, inc=1, **peer_of("fsdp", index))
    for index in ctx_peers:
        pl.semaphore_signal(barrier, inc=1, **peer_of("ctx", index))
    pl.semaphore_wait(barrier, len(fsdp_peers) + len(ctx_peers))

    def to_twin(i, step):
        return pltpu.make_async_remote_copy(
            src_ref=ins[i].at[ahead(step) * 2 + (1 - inner)],
            dst_ref=from_twin[i].at[step],
            send_sem=send.at[i, step],
            recv_sem=recv.at[i, step],
            **peer_of("fsdp", twin),
        )

    def to_owner(i, step):
        return pltpu.make_async_remote_copy(
            src_ref=paired[i].at[step],
            dst_ref=landed[i].at[step],
            send_sem=send.at[i, span + step],
            recv_sem=recv.at[i, span + step],
            **peer_of("fsdp", ahead(step) * 2 + inner),
        )

    def spread(i, slot, lane, target):
        return pltpu.make_async_remote_copy(
            src_ref=outs[i].at[slot],
            dst_ref=outs[i].at[slot],
            send_sem=send_ctx.at[i, lane],
            recv_sem=recv_ctx.at[i, lane],
            **peer_of("ctx", target),
        )

    def publish(i):
        for step in range(1, reach):
            spread(i, part, step, across(step)).start()
        spread(i, part, 0, mate).start()

    for i in range(sums):
        for step in list(range(1, span)) + [0]:
            to_twin(i, step).start()
    for i in range(sums, count):
        outs[i][part] = ins[i][...]
        publish(i)
    for i in range(sums):
        for step in range(1, span):
            to_twin(i, step).wait_recv()
            paired[i][step] = (
                ins[i][ahead(step) * 2 + inner].astype(f32) + from_twin[i][step].astype(f32)
            ).astype(paired[i].dtype)
            to_owner(i, step).start()
    for i in range(sums):
        to_twin(i, 0).wait_recv()
        total = ins[i][me].astype(f32) + from_twin[i][0].astype(f32)
        for step in range(1, span):
            to_owner(i, step).wait_recv()
            total = total + landed[i][step].astype(f32)
        outs[i][part] = total.astype(outs[i].dtype)
        publish(i)
    turn = list(range(sums, count)) + list(range(sums))
    for i in turn:
        for step in range(1, reach):
            slot = behind(step) * 2 + core
            spread(i, slot, step, mate).wait_recv()
            spread(i, slot, reach - 1 + step, mate).start()
    for i in turn:
        spread(i, mate, 0, mate).wait_recv()
        for step in range(1, reach):
            spread(i, behind(step) * 2 + (1 - core), reach - 1 + step, mate).wait_recv()
        for lane in range(2 * reach - 1):
            spread(i, part, lane, mate).wait_send()
    for i in range(sums):
        for step in range(span):
            to_twin(i, step).wait_send()
        for step in range(1, span):
            to_owner(i, step).wait_send()


def finish(owners, ways, key, summed, others):
    arrays = summed + others
    sums, count = len(summed), len(arrays)
    spec = pl.BlockSpec(memory_space=pltpu.VMEM)
    shapes = [(ways,) + a.shape[1:] for a in summed] + [(ways,) + a.shape for a in others]
    slots = [pltpu.VMEM((owners // 2,) + a.shape[1:], a.dtype) for a in summed]
    return pl.pallas_call(
        functools.partial(finish_kernel, owners, ways, sums, count),
        out_shape=[jax.ShapeDtypeStruct(shape, a.dtype) for shape, a in zip(shapes, arrays)],
        in_specs=[spec] * count,
        out_specs=[spec] * count,
        scratch_shapes=slots * 3
        + [pltpu.SemaphoreType.DMA((sums, owners))] * 2
        + [pltpu.SemaphoreType.DMA((count, ways - 1))] * 2,
        compiler_params=pltpu.CompilerParams(
            collective_id=key, has_side_effects=True, vmem_limit_bytes=VMEM_BYTES
        ),
    )(*arrays)


def turned_norm(values, gain_vec, cosine, sine_table):
    return rotate(rms_gain(values, gain_vec), cosine, sine_table)


def split_body(
    tokens,
    positions,
    cotangent,
    attn_norm,
    w_query,
    w_key,
    w_value,
    query_norm,
    key_norm,
    w_output,
    attn_post_norm,
    ffn_norm,
    w_gate,
    w_up,
    w_down,
    ffn_post_norm,
):
    f32 = jnp.float32
    bf16 = jnp.bfloat16
    ways = lax.axis_size("ctx")
    owners = lax.axis_size("fsdp")
    part = lax.axis_index("ctx")
    rows, width = tokens.shape[1:]
    seq = rows * ways
    shard = w_query.shape[0]
    hidden_row = w_down.shape[0] // ways
    out_row = w_output.shape[0] // ways
    head_share = query_norm.shape[0]
    hidden_cols = owners * hidden_row
    inputs = tokens.reshape(rows, width).astype(f32)
    grad_out = cotangent.reshape(rows, width).astype(f32)

    def mul(left, right, dims):
        return lax.dot_general(left, right, (dims, ((), ())), preferred_element_type=f32)

    def nn(left, right):
        return mul(left, right, ((1,), (0,)))

    def nt(left, right):
        return mul(left, right, ((1,), (1,)))

    def tn(left, right):
        return mul(left, right, ((0,), (0,)))

    def hidden_part(weight):
        cut = weight.reshape(shard, owners, ways, hidden_row)
        return lax.dynamic_index_in_dim(cut, part, 2, keepdims=False).reshape(
            shard, owners * hidden_row
        )

    def hidden_whole(parts):
        return (
            parts.reshape(ways, shard, owners, hidden_row)
            .transpose(1, 2, 0, 3)
            .reshape(shard, owners * ways * hidden_row)
        )

    gain_row = jnp.concatenate(
        [attn_norm, attn_post_norm, ffn_norm, ffn_post_norm, query_norm, key_norm]
    )
    gain_size = gain_row.shape[0]
    attn_pack = jnp.concatenate(
        [
            jnp.concatenate(
                [lax.dynamic_slice_in_dim(w_query, part * HD, HD, 1), w_key, w_value], axis=1
            ),
            jnp.pad(gain_row[None], ((0, 15), (0, 3 * HD - gain_size))),
        ],
        axis=0,
    )
    hidden_cols = owners * hidden_row
    attn_all, wo_rows = exchange(
        0,
        (Gather, "fsdp", attn_pack, bf16),
        (
            Gather,
            "fsdp",
            lax.dynamic_slice_in_dim(w_output, part * out_row, out_row, 0),
            bf16,
        ),
    )
    gains = attn_all[:, shard, :gain_size].astype(f32)

    def gain_of(index):
        return gains[:, index * shard : (index + 1) * shard].reshape(width)

    g_attn, g_post, g_ffn, g_ffn_post = (gain_of(index) for index in range(4))
    g_query = gains[:, 4 * shard : 4 * shard + head_share].reshape(HD)
    g_key = gains[:, 4 * shard + head_share :].reshape(HD)
    w_qkv = attn_all[:, :shard].reshape(width, 3 * HD)
    wq_head, wk_full, wv_full = (w_qkv[:, i * HD : (i + 1) * HD] for i in range(3))
    attn_in = rms_gain(inputs, g_attn).astype(bf16)
    attn_seq, place_all, wo_head, wg_all = exchange(
        2,
        (Gather, "ctx", attn_in, bf16),
        (Gather, "ctx", jnp.broadcast_to(positions.reshape(1, rows), (8, rows)), jnp.int32),
        (Swap, "ctx", wo_rows.reshape(ways, owners // ways * out_row, width), bf16),
        (Gather, "fsdp", hidden_part(w_gate), bf16),
    )
    wg_part = wg_all.reshape(width, hidden_cols)
    wo_head = (
        wo_head.reshape(ways, owners // ways, out_row, width)
        .transpose(1, 0, 2, 3)
        .reshape(HD, width)
    )
    attn_seq = attn_seq.reshape(seq, width)
    seq_place = place_all[:, 0].reshape(seq)
    index = jnp.arange(seq, dtype=jnp.int32)
    key_mask = (
        (index[None, :] <= index[:, None])
        & (index[:, None] - index[None, :] < WINDOW)
        & (index[None, :] >= (index - seq_place)[:, None])
    )
    cosine, sine_table = rope_tables(seq_place)
    cosine, sine_table = cosine[:, 0], sine_table[:, 0]
    qkv = nn(attn_seq, w_qkv)
    q_pre, k_pre, v_pre = (qkv[:, i * HD : (i + 1) * HD] for i in range(3))
    v_low = v_pre.astype(bf16)
    q_low = turned_norm(q_pre, g_query, cosine, sine_table).astype(bf16)
    k_low = turned_norm(k_pre, g_key, cosine, sine_table).astype(bf16)
    scores = jnp.where(key_mask, nt(q_low, k_low) * ATTN_SCALE, NEGATIVE)
    shifted = jnp.exp(scores - jnp.max(scores, axis=-1, keepdims=True))
    prob_rows = shifted / jnp.sum(shifted, axis=-1, keepdims=True)
    prob_low = prob_rows.astype(bf16)
    att_low = nn(prob_low, v_low).astype(bf16)

    def by_rows(value):
        return value.astype(bf16).reshape(ways, rows, value.shape[1])

    def blocks(value):
        return value.astype(bf16).reshape(owners, value.shape[0] // owners, value.shape[1])

    branch, wu_all = exchange(
        3,
        (Sum, "ctx", by_rows(nn(att_low, wo_head)), f32),
        (Gather, "fsdp", hidden_part(w_up), bf16),
    )
    wu_part = wu_all.reshape(width, hidden_cols)
    hidden_res = inputs + rms_gain(branch, g_post)
    ffn_seq, wd_all = exchange(
        4,
        (Gather, "ctx", rms_gain(hidden_res, g_ffn).astype(bf16), bf16),
        (
            Gather,
            "fsdp",
            lax.dynamic_slice_in_dim(w_down, part * hidden_row, hidden_row, 0),
            bf16,
        ),
    )
    ffn_seq = ffn_seq.reshape(seq, width)
    wd_part = wd_all.reshape(hidden_cols, width)
    gate_proj = nn(ffn_seq, wg_part)
    up_proj = nn(ffn_seq, wu_part)
    mixed_low = gated_gelu(gate_proj, up_proj).astype(bf16)
    (down_out,) = exchange(5, (Sum, "ctx", by_rows(nn(mixed_low, wd_part)), f32))
    layer_out = hidden_res + rms_gain(down_out, g_ffn_post)

    d_down, d_ffn_post = jax.vjp(rms_gain, down_out, g_ffn_post)[1](grad_out)
    d_down_seq = exchange(6, (Gather, "ctx", d_down.astype(bf16), bf16))[0].reshape(seq, width)
    d_mixed = nt(d_down_seq, wd_part)
    d_gate, d_up = jax.vjp(gated_gelu, gate_proj, up_proj)[1](d_mixed)
    d_gate_low = d_gate.astype(bf16)
    d_up_low = d_up.astype(bf16)
    d_ffn_in, wd_g = exchange(
        7,
        (Sum, "ctx", by_rows(nt(d_gate_low, wg_part) + nt(d_up_low, wu_part)), f32),
        (Sum, "fsdp", blocks(tn(mixed_low, d_down_seq)), bf16),
    )
    d_hidden_part, d_ffn_norm = jax.vjp(rms_gain, hidden_res, g_ffn)[1](d_ffn_in)
    d_hidden = grad_out + d_hidden_part

    d_branch, d_post = jax.vjp(rms_gain, branch, g_post)[1](d_hidden)
    d_branch_seq, wg_g = exchange(
        8,
        (Gather, "ctx", d_branch.astype(bf16), bf16),
        (Sum, "fsdp", blocks(tn(ffn_seq, d_gate_low)), bf16),
    )
    d_branch_seq = d_branch_seq.reshape(seq, width)
    grad_w_output = tn(att_low, d_branch_seq)
    d_att = nt(d_branch_seq, wo_head).astype(bf16)
    d_values = tn(prob_low, d_att)
    d_probs = nt(d_att, v_low)
    d_scores = prob_rows * (d_probs - jnp.sum(prob_rows * d_probs, axis=-1, keepdims=True))
    d_scores_low = d_scores.astype(bf16)
    d_queries = nn(d_scores_low, k_low) * ATTN_SCALE
    d_keys = tn(d_scores_low, q_low) * ATTN_SCALE
    d_q_pre, d_query_norm = jax.vjp(
        lambda values, gain_vec: turned_norm(values, gain_vec, cosine, sine_table), q_pre, g_query
    )[1](d_queries)
    dq_low = d_q_pre.astype(bf16)
    sums, wu_g = exchange(
        9,
        (
            Sum,
            "ctx",
            by_rows(jnp.concatenate([nt(dq_low, wq_head), d_keys, d_values], axis=1)),
            f32,
        ),
        (Sum, "fsdp", blocks(tn(ffn_seq, d_up_low)), bf16),
    )
    own_cos = lax.dynamic_slice_in_dim(cosine, part * rows, rows, 0)
    own_sin = lax.dynamic_slice_in_dim(sine_table, part * rows, rows, 0)
    own_k = lax.dynamic_slice_in_dim(k_pre, part * rows, rows, 0)
    d_k_pre, d_key_norm = jax.vjp(
        lambda values, gain_vec: turned_norm(values, gain_vec, own_cos, own_sin), own_k, g_key
    )[1](sums[:, width : width + HD])
    dkv_low = jnp.concatenate([d_k_pre, sums[:, width + HD :]], axis=1).astype(bf16)
    d_attn_in = sums[:, :width] + nt(dkv_low, w_qkv[:, HD:])
    dkv_seq, grad_wo_rows, wq_g = exchange(
        10,
        (Gather, "ctx", dkv_low, bf16),
        (
            Swap,
            "ctx",
            grad_w_output.astype(bf16)
            .reshape(owners // ways, ways, out_row, width)
            .transpose(1, 0, 2, 3)
            .reshape(ways, owners // ways * out_row, width),
            bf16,
        ),
        (Sum, "fsdp", blocks(tn(attn_seq, dq_low)), bf16),
    )
    dkv_seq = dkv_seq.reshape(seq, 2 * HD)
    grad_wo_rows = grad_wo_rows.reshape(owners, out_row, width)
    d_inputs_part, d_attn_norm = jax.vjp(rms_gain, inputs, g_attn)[1](d_attn_in)
    d_tokens = d_hidden + d_inputs_part
    dkv_cols = 2 * HD // ways
    grad_w_kv = tn(attn_seq, lax.dynamic_slice_in_dim(dkv_seq, part * dkv_cols, dkv_cols, 1))

    gain_grads = jnp.concatenate(
        [
            value.reshape(owners, -1)
            for value in (d_attn_norm, d_post, d_ffn_norm, d_ffn_post, d_query_norm, d_key_norm)
        ],
        axis=1,
    )
    gain_grads = jnp.pad(gain_grads[:, None], ((0, 0), (0, 15), (0, 0)))

    wo_g, wkv_g, gain_g, wg_g, wu_g, wd_g, wq_g = finish(
        owners,
        ways,
        12,
        [grad_wo_rows, blocks(grad_w_kv), gain_grads.astype(bf16)],
        [wg_g, wu_g, wd_g, wq_g],
    )
    gain_sum = jnp.sum(gain_g[:, 0].astype(f32), axis=0)
    ends = [shard * i for i in range(1, 5)] + [4 * shard + head_share]
    t_attn, t_post, t_ffn, t_ffn_post, t_query, t_key = jnp.split(gain_sum, ends)
    half = ways // 2

    def columns(parts):
        return parts.transpose(1, 0, 2).reshape(shard, -1).astype(f32)

    return (
        layer_out.astype(bf16).reshape(1, rows, width),
        d_tokens.astype(bf16).reshape(1, rows, width),
        t_attn,
        columns(wq_g),
        columns(wkv_g[:half]),
        columns(wkv_g[half:]),
        t_query,
        t_key,
        wo_g.reshape(ways * out_row, width).astype(f32),
        t_post,
        t_ffn,
        hidden_whole(wg_g).astype(f32),
        hidden_whole(wu_g).astype(f32),
        wd_g.reshape(ways * hidden_row, width).astype(f32),
        t_ffn_post,
    )


def solution(mesh):
    return jax.shard_map(
        plain_body if mesh.shape['ctx'] != HQ or mesh.shape['fsdp'] != 2 * HQ else split_body,
        mesh=mesh,
        in_specs=(
            P("fsdp", "ctx", None),
            P("fsdp", "ctx"),
            P("fsdp", "ctx", None),
            P("fsdp"),
            P("fsdp", None),
            P("fsdp", None),
            P("fsdp", None),
            P("fsdp"),
            P("fsdp"),
            P("fsdp", None),
            P("fsdp"),
            P("fsdp"),
            P("fsdp", None),
            P("fsdp", None),
            P("fsdp", None),
            P("fsdp"),
        ),
        out_specs=(
            P("fsdp", "ctx", None),
            P("fsdp", "ctx", None),
            P("fsdp"),
            P("fsdp", None),
            P("fsdp", None),
            P("fsdp", None),
            P("fsdp"),
            P("fsdp"),
            P("fsdp", None),
            P("fsdp"),
            P("fsdp"),
            P("fsdp", None),
            P("fsdp", None),
            P("fsdp", None),
            P("fsdp"),
        ),
        check_vma=False,
    )
```
